512 devices in a mesh: heads: 8 (over z), seq: 64 (over y, x, core).
Axes of the slice: x: 4, y: 8, z: 8, core: 2. Of those that a mesh axis runs over, the one named last changes fastest.
Arguments:
- tokens: bfloat16 [16, 16384], P(None, 'seq')
- norm_gain: bfloat16 [16384], P('seq'), may hold values from 0.099609375 to 1.8984375
- w_query: bfloat16 [16384, 16384], P('seq', 'heads'), may hold values from -0.046875 to 0.046875
- w_kv: bfloat16 [16384, 2048], P('seq', 'heads'), may hold values from -0.046875 to 0.046875
- w_out: bfloat16 [16384, 16384], P('heads', 'seq'), may hold values from -0.125 to 0.125
- key_cache: bfloat16 [8, 16, 16384, 128], P('heads', None, 'seq')
- value_cache: bfloat16 [8, 16, 16384, 128], P('heads', None, 'seq'), may hold values from -6 to 6
- lengths: int32 [16], replicated, may hold values from 1 to 16384, as said below
- positions: int32 [16], replicated, may hold values from 0 to 8191
Outputs:
- outputs: float32 [2, 16, 16384], P(None, None, 'seq')
The draws below stay inside these ranges and needn't reach their ends.
Inputs may be any that keep to these rules, and one draw needn't show every extreme that they name: `lengths`: some row has all 16384 cached positions valid in every draw.
All inputs are finite; a program needn't handle non-finite values.
Results may differ from the reference program's by a relative error of at most 0.028.
Values sent between devices are 32-bit elements; how exact they have to be, the bound alone decides.
No kernel may reach another device: no remote copies, remote signals or barrier semaphores. Data moves between devices by JAX's collectives and lax.ppermute only.
A program may use at most 64 MiB of HBM per device.

```python
import math
import jax
import jax.numpy as jnp
from jax import lax

D = 16384
GROUP_HEADS = 16
HEAD_DIM = 128
KV_HEADS = 8
ROWS = 16
STEPS = 2
SEQ_LEN = 16384


def draw_tokens(key, part):
    key = jax.random.fold_in(key, 11)
    base_key, row_key = jax.random.split(key)
    ramp = 10.0 ** (jnp.arange(D, dtype=jnp.float32) / D)
    base = jax.random.normal(base_key, (ROWS, D), jnp.float32)
    row_scale = jnp.exp(jax.random.uniform(row_key, (ROWS, 1), jnp.float32) * jnp.log(10.0))
    return (base * ramp[None, :] * row_scale).astype(jnp.bfloat16)


def draw_key_cache(key, part):
    key = jax.random.fold_in(key, 23)
    base_key = jax.random.fold_in(key, 0)
    shape = (KV_HEADS, ROWS, SEQ_LEN, HEAD_DIM)
    return (2.0 * jax.random.normal(base_key, shape, jnp.float32)).astype(jnp.bfloat16)


def draw_lengths(key, part):
    key = jax.random.fold_in(key, 37)
    power_key, row_key = jax.random.split(key)
    powers = jax.random.randint(power_key, (ROWS,), 0, 11)
    chosen = jax.random.randint(row_key, (), 0, ROWS)
    powers = jnp.where(jnp.arange(ROWS) == chosen, 0, powers)
    return jnp.maximum(1, SEQ_LEN // jnp.left_shift(1, powers)).astype(jnp.int32)


def place_ends(entries, stream_key, low, top_value):
    longest = entries.shape.index(max(entries.shape))
    spots = []
    for shift in (0, 1):
        where = [jax.random.randint(jax.random.fold_in(stream_key, axis), (), 0, length) for axis, length in enumerate(entries.shape)]
        where[longest] = (where[longest] + shift) % entries.shape[longest]
        spots.append(tuple(where))
    return entries.at[spots[0]].set(low).at[spots[1]].set(top_value)


def block_levels(own_key, shape, pieces, least, largest):
    loudness, own = 1.0, jax.random.fold_in(own_key, 6)
    for position, blocks in pieces:
        heights = jnp.exp(jax.random.uniform(jax.random.fold_in(own, position), (blocks,), jnp.float32, least / len(pieces), largest / len(pieces)))
        loudness = loudness * jnp.repeat(heights, shape[position] // blocks).reshape([-1 if axis == position else 1 for axis in range(len(shape))])
    return loudness


def gaussian(stream_key, extent, width, limit, cuts=(), kind=jnp.bfloat16):
    values = jax.random.normal(stream_key, extent, jnp.float32) * width
    if len(cuts) > 0:
        values = block_levels(stream_key, extent, cuts, -0.22, 0.18) * values
    return jnp.clip(values, min=-limit, max=limit).astype(kind)


def setup_inputs(seed: int = 0) -> dict:
    keys = jax.random.split(jax.random.key(seed), 10)
    return {
        "tokens": draw_tokens(jax.random.fold_in(keys[9], 71), 0),
        "norm_gain": jnp.clip(1.0 + 0.18 * jax.random.normal(keys[1], (D,), jnp.float32), 0.099609375, 1.8984375).astype(jnp.bfloat16),
        "w_query": gaussian(keys[2], (D, KV_HEADS * GROUP_HEADS * HEAD_DIM), D ** -0.5, 0.046875, ((0, 64), (1, 8))),
        "w_kv": gaussian(keys[3], (D, KV_HEADS * 2 * HEAD_DIM), D ** -0.5, 0.046875, ((0, 64), (1, 8))),
        "w_out": gaussian(keys[4], (KV_HEADS * GROUP_HEADS * HEAD_DIM, D), (GROUP_HEADS * HEAD_DIM) ** -0.5, 0.125, ((0, 8), (1, 64))),
        "key_cache": draw_key_cache(jax.random.fold_in(keys[9], 71), 0),
        "value_cache": gaussian(keys[6], (KV_HEADS, ROWS, SEQ_LEN, HEAD_DIM), 1.0, 6.0, ((0, 8), (2, 64))),
        "lengths": draw_lengths(jax.random.fold_in(keys[9], 71), 0),
        "positions": place_ends(jax.random.randint(keys[8], (ROWS,), 0, 8192), jax.random.fold_in(keys[8], 1), 0, 8191).astype(jnp.int32),
    }


EPSILON = 1e-05
ROPE_BASE = 500000.0

def rotary(vectors, places):
    half_width = vectors.shape[-1] // 2
    freqs = ROPE_BASE ** (-(jnp.arange(half_width, dtype=jnp.float32) * 2.0 / vectors.shape[-1]))
    angles = places.astype(jnp.float32)[:, None] * freqs[None, :]
    angles = angles.reshape(angles.shape[:1] + (1,) * (vectors.ndim - 2) + angles.shape[1:])
    cosine = jnp.cos(angles)
    sine = jnp.sin(angles)
    first = vectors[..., :half_width]
    second = vectors[..., half_width:]
    return jnp.concatenate([first * cosine - second * sine, second * cosine + first * sine], axis=-1)

def reference(tokens, norm_gain, w_query, w_kv, w_out, key_cache, value_cache, lengths, positions):
    scale = 1.0 / math.sqrt(HEAD_DIM)
    visible = jnp.arange(SEQ_LEN, dtype=jnp.int32)[None, :] < lengths[:, None]
    state = tokens
    own_keys = []
    own_values = []
    results = []
    for decode_step in range(STEPS):
        wide = state.astype(jnp.float32)
        squares = lax.optimization_barrier(jnp.sum(wide * wide, axis=1))
        inverse = lax.rsqrt(squares / D + EPSILON)
        gained = (wide * norm_gain.astype(jnp.float32)).astype(jnp.bfloat16)
        query_raw = jnp.dot(gained, w_query, preferred_element_type=jnp.float32) * inverse[:, None]
        kv_raw = jnp.dot(gained, w_kv, preferred_element_type=jnp.float32) * inverse[:, None]
        places = positions + decode_step
        queries = rotary(query_raw.reshape(ROWS, KV_HEADS, GROUP_HEADS, HEAD_DIM), places).astype(jnp.bfloat16)
        kv_raw = kv_raw.reshape(ROWS, KV_HEADS, 2, HEAD_DIM)
        own_keys.append(rotary(kv_raw[:, :, 0], places).astype(jnp.bfloat16))
        own_values.append(kv_raw[:, :, 1].astype(jnp.bfloat16))
        fresh_keys = jnp.stack(own_keys, 0).transpose(2, 0, 1, 3)
        fresh_values = jnp.stack(own_values, 0).transpose(2, 0, 1, 3)

        def one_group(group):
            group_queries, group_keys, group_values, new_keys, new_values = group
            query_wide = group_queries.astype(jnp.float32)
            scores = jnp.einsum('bjd,btd->bjt', query_wide, group_keys.astype(jnp.float32)) * scale
            scores = jnp.where(visible[:, None, :], scores, -jnp.inf)
            new_scores = jnp.einsum('bjd,nbd->bjn', query_wide, new_keys.astype(jnp.float32)) * scale
            top = jnp.maximum(lax.optimization_barrier(jnp.max(scores, axis=-1)), lax.optimization_barrier(jnp.max(new_scores, axis=-1)))
            probs = jnp.where(visible[:, None, :], jnp.exp(scores - top[..., None]), 0.0)
            new_probs = jnp.exp(new_scores - top[..., None])
            total = lax.optimization_barrier(jnp.sum(probs, axis=-1)) + lax.optimization_barrier(jnp.sum(new_probs, axis=-1))
            rounded = lax.optimization_barrier(probs.astype(jnp.bfloat16)).astype(jnp.float32)
            new_rounded = lax.optimization_barrier(new_probs.astype(jnp.bfloat16)).astype(jnp.float32)
            weighted = jnp.einsum('bjt,btd->bjd', rounded, group_values.astype(jnp.float32))
            weighted = weighted + jnp.einsum('bjn,nbd->bjd', new_rounded, new_values.astype(jnp.float32))
            return (weighted / total[..., None]).astype(jnp.bfloat16)
        attended = lax.map(one_group, (queries.transpose(1, 0, 2, 3), key_cache, value_cache, fresh_keys, fresh_values))
        attended = attended.transpose(1, 0, 2, 3).reshape(ROWS, KV_HEADS * GROUP_HEADS * HEAD_DIM)
        output = jnp.dot(attended, w_out, preferred_element_type=jnp.float32)
        results.append(output)
        state = (wide + output).astype(jnp.bfloat16)
    return jnp.stack(results, 0)
```

```python
import math

import jax
import jax.numpy as jnp
from jax import lax
from jax.sharding import Mesh, PartitionSpec as P

D = 16384
STEPS = 2
EPSILON = 1e-05
ROPE_BASE = 500000.0
FILLER = -3e38
CHIPS_Y = 8
INNER = ("x", "core")
SEQ = ("y", "x", "core")


def scatter(pieces, axes):
    return lax.all_to_all(pieces, axes, 0, 0, tiled=True)


def gather(piece, axes, size):
    copies = jnp.broadcast_to(piece[None], (size,) + piece.shape)
    return lax.all_to_all(copies, axes, 0, 0, tiled=True)


def angles_of(places, head_dim):
    half = head_dim // 2
    freqs = ROPE_BASE ** (-(jnp.arange(half, dtype=jnp.float32) * 2.0 / head_dim))
    angles = places.astype(jnp.float32)[:, None] * freqs[None, :]
    return jnp.cos(angles)[:, None], jnp.sin(angles)[:, None]


def rotary(vectors, cosine, sine):
    half = vectors.shape[-1] // 2
    first = vectors[..., :half]
    second = vectors[..., half:]
    return jnp.concatenate(
        [first * cosine - second * sine, second * cosine + first * sine], axis=-1
    )


def per_device(sizes, tokens, norm_gain, w_query, w_kv, w_out, key_cache, value_cache, lengths, positions):
    heads_size, y_size, inner_size = sizes
    rows = tokens.shape[0]
    seq_here = key_cache.shape[2]
    head_dim = key_cache.shape[3]
    group_heads = w_query.shape[1] // head_dim
    rows_own = rows // inner_size
    scale = 1.0 / math.sqrt(head_dim)
    keys_local = key_cache[0]
    values_local = value_cache[0]
    offset = lax.axis_index(SEQ) * seq_here
    visible = (offset + jnp.arange(seq_here, dtype=jnp.int32))[None, :] < lengths[:, None]
    visible = visible[:, None, :]
    inner = lax.axis_index(INNER)
    own_positions = lax.dynamic_slice(positions, (inner * rows_own,), (rows_own,))
    gain_wide = norm_gain.astype(jnp.float32)
    state = tokens
    own_keys = []
    own_values = []
    results = []
    for decode_step in range(STEPS):
        wide = state.astype(jnp.float32)
        gained = (wide * gain_wide[None, :]).astype(jnp.bfloat16)
        squares = jnp.broadcast_to(jnp.sum(wide * wide, axis=1)[:, None], (rows, head_dim))
        projected = jnp.concatenate(
            [
                jnp.dot(gained, w_query, preferred_element_type=jnp.float32),
                jnp.dot(gained, w_kv, preferred_element_type=jnp.float32),
                squares,
            ],
            axis=1,
        )
        width = projected.shape[1]
        part = scatter(projected.reshape(inner_size, rows_own, width), INNER)
        part = gather(jnp.sum(part, axis=0), ("y",), y_size)
        part = jnp.sum(part, axis=0)
        inverse = lax.rsqrt(part[:, width - head_dim :] / D + EPSILON)
        cosine, sine = angles_of(own_positions + decode_step, head_dim)
        raw = part[:, : width - head_dim].reshape(rows_own, group_heads + 2, head_dim)
        vectors = raw * inverse[:, None]
        turned = rotary(vectors[:, : group_heads + 1], cosine, sine)
        own_keys.append(turned[:, group_heads].astype(jnp.bfloat16))
        own_values.append(vectors[:, group_heads + 1].astype(jnp.bfloat16))
        queries_own = turned[:, :group_heads]
        sent = jnp.concatenate([rotary(raw[:, :group_heads], cosine, sine), inverse[:, None]], axis=1)
        sent = gather(sent, INNER, inner_size).reshape(rows, group_heads + 1, head_dim)
        queries = (sent[:, :group_heads] * sent[:, group_heads:]).astype(jnp.bfloat16)
        scores = (
            jnp.einsum("bjd,btd->bjt", queries, keys_local, preferred_element_type=jnp.float32)
            * scale
        )
        top = jnp.max(jnp.where(visible, scores, FILLER), axis=-1)
        probs = jnp.where(visible, jnp.exp(scores - top[..., None]), 0.0)
        total = jnp.sum(probs, axis=-1)
        weighted = jnp.einsum(
            "bjt,btd->bjd",
            probs.astype(jnp.bfloat16),
            values_local,
            preferred_element_type=jnp.float32,
        )

        def send(top, total, weighted, axes, count):
            lead = weighted.shape[:-3] if axes == INNER else ()
            stats = jnp.stack([top, total], axis=1)
            stats = jnp.pad(stats, ((0, 0), (0, 0), (0, head_dim - group_heads)))
            block = jnp.concatenate([weighted, stats], axis=1)
            if axes == INNER:
                got = scatter(block.reshape(inner_size, rows_own, group_heads + 2, head_dim), axes)
            else:
                got = gather(block, axes, count)
            tops = got[:, :, group_heads, :group_heads]
            totals = got[:, :, group_heads + 1, :group_heads]
            top = jnp.max(tops, axis=0)
            factor = jnp.exp(tops - top[None])
            total = jnp.sum(factor * totals, axis=0)
            weighted = jnp.sum(factor[..., None] * got[:, :, :group_heads], axis=0)
            return top, total, weighted

        top, total, weighted = send(top, total, weighted, INNER, inner_size)
        top, total, weighted = send(top, total, weighted, ("y",), y_size)
        own_queries = queries_own.astype(jnp.bfloat16)
        fresh_keys = jnp.stack(own_keys, 1)
        fresh_values = jnp.stack(own_values, 1)
        new_scores = (
            jnp.einsum("bjd,bnd->bjn", own_queries, fresh_keys, preferred_element_type=jnp.float32)
            * scale
        )
        whole_top = jnp.maximum(top, jnp.max(new_scores, axis=-1))
        factor = jnp.exp(top - whole_top)
        new_probs = jnp.exp(new_scores - whole_top[..., None])
        total = total * factor + jnp.sum(new_probs, axis=-1)
        weighted = weighted * factor[..., None] + jnp.einsum(
            "bjn,bnd->bjd",
            new_probs.astype(jnp.bfloat16),
            fresh_values,
            preferred_element_type=jnp.float32,
        )
        stats = jnp.pad(total, ((0, 0), (0, head_dim - group_heads)))
        sent = jnp.concatenate([weighted, stats[:, None]], axis=1)
        sent = gather(sent, INNER, inner_size).reshape(rows, group_heads + 1, head_dim)
        attended = sent[:, :group_heads] / sent[:, group_heads, :group_heads][..., None]
        attended = attended.reshape(rows, group_heads * head_dim).astype(jnp.bfloat16)
        partial_out = jnp.dot(attended, w_out, preferred_element_type=jnp.float32)
        output = jnp.sum(gather(partial_out, ("heads",), heads_size), axis=0)
        results.append(output)
        state = (wide + output).astype(jnp.bfloat16)
    return jnp.stack(results, 0)


def solution(mesh):
    heads_size = mesh.shape["heads"]
    seq_size = mesh.shape["seq"]
    inner_size = seq_size // CHIPS_Y
    devices = mesh.devices.reshape(heads_size, CHIPS_Y, inner_size // 2, 2)
    fine = Mesh(devices, ("heads", "y", "x", "core"))
    in_specs = (
        P(None, SEQ),
        P(SEQ),
        P(SEQ, "heads"),
        P(SEQ, "heads"),
        P("heads", SEQ),
        P("heads", None, SEQ, None),
        P("heads", None, SEQ, None),
        P(),
        P(),
    )

    def body(*args):
        return per_device((heads_size, CHIPS_Y, inner_size), *args)

    return jax.shard_map(
        body, mesh=fine, in_specs=in_specs, out_specs=P(None, None, SEQ), check_vma=False
    )
```

```python
import functools
import math

import jax
import jax.numpy as jnp
from jax import lax
from jax.experimental import pallas as pl
from jax.experimental.pallas import tpu as pltpu
from jax.sharding import Mesh, PartitionSpec as P

D = 16384
STEPS = 2
EPSILON = 1e-05
ROPE_BASE = 500000.0
FILLER = -3e38
CHIPS_Y = 8
INNER = ("x", "core")
SEQ = ("y", "x", "core")

ROWS = 16
HEADS = 16
DIM = 128
GROUP = 8
OWN = ROWS // GROUP
PIECE = 40
BATCH = 4
CHUNKS = 4
SCALE = 1.0 / math.sqrt(DIM)
F32 = jnp.float32
BF16 = jnp.bfloat16


def kernel_call(body, out_shapes, *args, scratch=(), space=pltpu.VMEM):
    single = not isinstance(out_shapes, (list, tuple))
    vmem = pl.BlockSpec(memory_space=pltpu.VMEM)
    return pl.pallas_call(
        body,
        out_shape=out_shapes,
        in_specs=[pl.BlockSpec(memory_space=space)] * len(args),
        out_specs=vmem if single else [vmem] * len(out_shapes),
        scratch_shapes=list(scratch),
        compiler_params=pltpu.CompilerParams(vmem_limit_bytes=16 * 1024 * 1024),
    )(*args)


def shape(*dims):
    return jax.ShapeDtypeStruct(dims, F32)


def project(wide, gain_ref, wq_ref, wkv_ref, pieces_ref, waits=None):
    gained = (wide * gain_ref[0:1, :]).astype(BF16)

    def put(row, block):
        for r in range(OWN):
            pieces_ref[pl.ds(row(r), GROUP, stride=PIECE), :] = block[r * GROUP : (r + 1) * GROUP]

    for j in range(HEADS // 2):
        if waits:
            waits[j]()
        both = jnp.dot(gained, wq_ref[:, 2 * j * DIM : 2 * (j + 1) * DIM], preferred_element_type=F32)
        for k in range(2):
            put(lambda r: r * HEADS + 2 * j + k, both[:, k * DIM : (k + 1) * DIM])
    if waits:
        waits[-1]()
    both = jnp.dot(gained, wkv_ref[...], preferred_element_type=F32)
    put(lambda r: 2 * HEADS + r, both[:, :DIM])
    put(lambda r: 2 * HEADS + OWN + r, both[:, DIM:])
    squares = jnp.broadcast_to(jnp.sum(wide * wide, axis=1, keepdims=True), (ROWS, DIM))
    put(lambda r: 2 * HEADS + 2 * OWN + r, squares)
    put(lambda r: 2 * HEADS + 3 * OWN + r, jnp.zeros((ROWS, DIM), F32))


def first_kernel(
    tokens_hbm, gain_hbm, wq_hbm, wkv_hbm, lengths_hbm, positions_hbm,
    pieces_ref, wide_ref, gain_ref, seen_ref, *refs,
):
    table_refs, (tokens_ref, gain_in, wq_ref, wkv_ref, lengths_ref, positions_ref, left_ref, right_ref, sems) = (
        refs[:STEPS], refs[STEPS:],
    )
    chunk = wq_ref.shape[1] // CHUNKS
    pairs = [
        (lengths_hbm, lengths_ref),
        (positions_hbm, positions_ref),
        (tokens_hbm, tokens_ref),
        (gain_hbm, gain_in),
        (wkv_hbm, wkv_ref),
    ]
    columns = [pl.ds(c * chunk, chunk) for c in range(CHUNKS)]
    pairs += [(wq_hbm.at[:, c], wq_ref.at[:, c]) for c in columns]
    copies = [pltpu.make_async_copy(a, b, sems.at[i]) for i, (a, b) in enumerate(pairs)]
    for copy in copies:
        copy.start()
    inner = lax.axis_index("x") * 2 + lax.axis_index("core")
    seq_here = seen_ref.shape[1]
    spot = (lax.axis_index("y") * GROUP + inner) * seq_here + lax.broadcasted_iota(jnp.int32, (1, seq_here), 1)
    copies[0].wait()
    copies[1].wait()
    for b in range(ROWS):
        seen_ref[b : b + 1, :] = jnp.where(spot < lengths_ref[b], 1.0, 0.0)
    lane = lax.broadcasted_iota(jnp.int32, (8, DIM), 1)
    line = lax.broadcasted_iota(jnp.int32, (8, DIM), 0)
    index = jnp.where(lane < DIM // 2, lane, lane - DIM // 2).astype(F32)
    freqs = jnp.exp(index * (-2.0 * math.log(ROPE_BASE) / DIM))
    place = jnp.where(line % 2 == 1, positions_ref[inner * OWN + 1], positions_ref[inner * OWN])
    for step, ref in enumerate(table_refs):
        angles = (place + step).astype(F32) * freqs
        sine = jnp.sin(angles)
        ref[...] = jnp.where(line < OWN, jnp.cos(angles), jnp.where(lane < DIM // 2, -sine, sine))
    copies[2].wait()
    copies[3].wait()
    width = tokens_ref.shape[1] // 2
    left_ref[...] = tokens_ref[:, :width].astype(F32)
    right_ref[...] = tokens_ref[:, width:].astype(F32)
    wide = jnp.concatenate(
        [
            jnp.concatenate([ref[pl.ds(r, GROUP, stride=OWN), :] for r in range(OWN)], axis=0)
            for ref in (left_ref, right_ref)
        ],
        axis=1,
    )
    wide_ref[...] = wide
    gain_ref[...] = jnp.broadcast_to(gain_in[...].astype(F32).reshape(1, 2 * width), gain_ref.shape)
    waits = [lambda j=j: copies[5 + j * 2 * DIM // chunk].wait() if j * 2 * DIM % chunk == 0 else None for j in range(HEADS // 2)]
    project(wide, gain_ref, wq_ref, wkv_ref, pieces_ref, waits + [copies[4].wait])


def next_kernel(sums_ref, last_ref, gain_ref, wq_ref, wkv_ref, pieces_ref, output_ref):
    output = sums_ref[0]
    for s in range(1, GROUP):
        output = output + sums_ref[s]
    output_ref[...] = output
    wide = (last_ref[...] + output).astype(BF16).astype(F32)
    project(wide, gain_ref, wq_ref, wkv_ref, pieces_ref)


def last_kernel(sums_ref, first_ref, result_ref):
    output = sums_ref[0]
    for s in range(1, GROUP):
        output = output + sums_ref[s]
    for step, value in enumerate((first_ref[...], output)):
        for b in range(ROWS):
            at = b % OWN * GROUP + b // OWN
            result_ref[step, b : b + 1, :] = value[at : at + 1, :]


def turn_kernel(parts_ref, table_ref, pieces_ref, own_ref):
    whole = parts_ref[0]
    for s in range(1, GROUP):
        whole = whole + parts_ref[s]
    table = table_ref[...]
    below = whole[2 * HEADS :]
    first = 2 * OWN
    inverse = [lax.rsqrt(below[first + r : first + r + 1] / D + EPSILON) for r in range(OWN)]
    cosine = [table[r : r + 1] for r in range(OWN)]
    sine = [table[OWN + r : OWN + r + 1] for r in range(OWN)]
    blocks = []
    for r in range(OWN):
        scaled = whole[r * HEADS : (r + 1) * HEADS] * inverse[r]
        blocks.append(scaled * cosine[r] + pltpu.roll(scaled, DIM // 2, 1) * sine[r])
    line = lax.broadcasted_iota(jnp.int32, below.shape, 0)
    odd = line % 2 == 1
    scaled = below * jnp.where(odd, inverse[1], inverse[0])
    cosines = jnp.where(line < OWN, jnp.where(odd, cosine[1], cosine[0]), 1.0)
    sines = jnp.where(line < OWN, jnp.where(odd, sine[1], sine[0]), 0.0)
    blocks.append(scaled * cosines + pltpu.roll(scaled, DIM // 2, 1) * sines)
    piece = jnp.concatenate(blocks, axis=0)
    own_ref[...] = piece
    for d in range(GROUP):
        pieces_ref[d] = piece


def diagonal():
    shape_here = (2 * HEADS, DIM)
    return lax.broadcasted_iota(jnp.int32, shape_here, 0) == lax.broadcasted_iota(jnp.int32, shape_here, 1)


def to_lanes(column):
    return jnp.sum(jnp.where(diagonal(), column, 0.0), axis=0, keepdims=True)


def to_column(line):
    return jnp.sum(jnp.where(diagonal(), line, 0.0), axis=1, keepdims=True)


def stats_block(top, total):
    line = lax.broadcasted_iota(jnp.int32, (PIECE - 2 * HEADS, DIM), 0)
    return jnp.where(line == 0, top, jnp.where(line == 1, total, 0.0))


def attend_kernel(queries_ref, keys_ref, values_ref, seen_ref, pieces_ref, work_ref):
    def place(b):
        return b // OWN, slice(b % OWN * HEADS, (b % OWN + 1) * HEADS)

    for b in range(ROWS):
        d, heads = place(b)
        queries = queries_ref[d, heads, :].astype(BF16)
        work_ref[b] = lax.dot_general(queries, keys_ref[b], (((1,), (1,)), ((), ())), preferred_element_type=F32)
    for c in range(0, ROWS, BATCH):
        scores = work_ref[c : c + BATCH] * SCALE
        seen = jnp.broadcast_to(seen_ref[c : c + BATCH, :][:, None, :], scores.shape) > 0.0
        tops = jnp.max(jnp.where(seen, scores, FILLER), axis=2, keepdims=True)
        probs = jnp.where(seen, jnp.exp(scores - tops), 0.0)
        totals = jnp.sum(probs, axis=2, keepdims=True)
        work_ref[c : c + BATCH] = probs
        for b in range(0, BATCH, OWN):
            top = tops[b : b + OWN].reshape(OWN * HEADS, 1)
            total = totals[b : b + OWN].reshape(OWN * HEADS, 1)
            pieces_ref[(c + b) // OWN, 2 * HEADS :, :] = stats_block(to_lanes(top), to_lanes(total))
    for b in range(ROWS):
        d, heads = place(b)
        pieces_ref[d, heads, :] = jnp.dot(work_ref[b].astype(BF16), values_ref[b], preferred_element_type=F32)


def merge(parts_ref):
    tops = [parts_ref[s, 2 * HEADS : 2 * HEADS + 1, :] for s in range(GROUP)]
    top = functools.reduce(jnp.maximum, tops)
    total, weighted = None, None
    for s in range(GROUP):
        factor = jnp.exp(tops[s] - top)
        here = factor * parts_ref[s, 2 * HEADS + 1 : 2 * HEADS + 2, :]
        part = to_column(factor) * parts_ref[s, : 2 * HEADS, :]
        total = here if total is None else total + here
        weighted = part if weighted is None else weighted + part
    return top, total, weighted


def merge_kernel(parts_ref, pieces_ref):
    top, total, weighted = merge(parts_ref)
    stats = stats_block(top, total)
    for d in range(GROUP):
        pieces_ref[d, : 2 * HEADS, :] = weighted
        pieces_ref[d, 2 * HEADS :, :] = stats


def finish_kernel(parts_ref, *refs):
    own_refs, pieces_ref = refs[:-1], refs[-1]

    def rounded(value):
        return value.astype(BF16).astype(F32)

    def spread(ref, line):
        return jnp.concatenate(
            [jnp.broadcast_to(rounded(ref[line + r : line + r + 1, :]), (HEADS, DIM)) for r in range(OWN)], axis=0
        )

    top, total, weighted = merge(parts_ref)
    top, total = to_column(top), to_column(total)
    queries = rounded(own_refs[-1][: 2 * HEADS, :])
    scores = [jnp.sum(queries * spread(ref, 2 * HEADS), axis=1, keepdims=True) * SCALE for ref in own_refs]
    whole_top = functools.reduce(jnp.maximum, scores, top)
    factor = jnp.exp(top - whole_top)
    total = total * factor
    weighted = weighted * factor
    for score, ref in zip(scores, own_refs):
        prob = jnp.exp(score - whole_top)
        total = total + prob
        weighted = weighted + rounded(prob) * spread(ref, 2 * HEADS + OWN)
    attended = weighted / total
    for d in range(GROUP):
        pieces_ref[d] = attended


def out_kernel(attended_ref, wout_ref, pieces_ref):
    partial = None
    for j in range(HEADS // 2):
        heads = jnp.concatenate(
            [
                jnp.concatenate(
                    [attended_ref[pl.ds(r * HEADS + 2 * j + k, GROUP, stride=2 * HEADS), :] for r in range(OWN)], axis=0
                )
                for k in range(2)
            ],
            axis=1,
        ).astype(BF16)
        term = jnp.dot(heads, wout_ref[2 * j * DIM : 2 * (j + 1) * DIM, :], preferred_element_type=F32)
        partial = term if partial is None else partial + term
    for d in range(GROUP):
        pieces_ref[d] = partial


def exchange(pieces, axes):
    return lax.all_to_all(pieces, axes, 0, 0, tiled=True)


def per_device(tokens, norm_gain, w_query, w_kv, w_out, key_cache, value_cache, lengths, positions):
    seq_here = key_cache.shape[2]
    width = tokens.shape[1]
    keys, values = key_cache[0], value_cache[0]
    flat = shape(GROUP * PIECE, DIM)
    cube = shape(GROUP, PIECE, DIM)
    half = pltpu.VMEM((ROWS, width // 2), F32)
    work = pltpu.VMEM((ROWS, HEADS, seq_here), F32)
    line = shape(8, DIM)
    pieces, wide, gain, seen, *tables = kernel_call(
        first_kernel,
        [flat, shape(ROWS, width), shape(8, width), shape(ROWS, seq_here)] + [line] * STEPS,
        *[
            pltpu.with_memory_space_constraint(array, pltpu.HBM)
            for array in (tokens, norm_gain, w_query, w_kv, lengths, positions)
        ],
        scratch=[
            pltpu.VMEM(tokens.shape, BF16),
            pltpu.VMEM(norm_gain.shape, BF16),
            pltpu.VMEM(w_query.shape, BF16),
            pltpu.VMEM(w_kv.shape, BF16),
            pltpu.SMEM(lengths.shape, jnp.int32),
            pltpu.SMEM(positions.shape, jnp.int32),
            half,
            half,
            pltpu.SemaphoreType.DMA((5 + CHUNKS,)),
        ],
        space=pltpu.HBM,
    )
    own, output = [], None
    for step in range(STEPS):
        if step:
            pieces, output = kernel_call(
                next_kernel, [flat, shape(ROWS, width)], sums, wide, gain, w_query, w_kv
            )
        parts = exchange(pieces.reshape(GROUP, PIECE, DIM), INNER)
        total = jnp.broadcast_to(jnp.sum(parts, axis=0)[None], (GROUP, PIECE, DIM))
        parts = exchange(total, ("y",))
        pieces, mine = kernel_call(turn_kernel, [cube, shape(PIECE, DIM)], parts, tables[step])
        own.append(mine)
        queries = exchange(pieces, INNER)
        parts = exchange(kernel_call(attend_kernel, cube, queries, keys, values, seen, scratch=[work]), INNER)
        parts = exchange(kernel_call(merge_kernel, cube, parts), ("y",))
        pieces = kernel_call(finish_kernel, shape(GROUP, 2 * HEADS, DIM), parts, *own)
        attended = exchange(pieces, INNER).reshape(GROUP * 2 * HEADS, DIM)
        sums = exchange(kernel_call(out_kernel, shape(GROUP, ROWS, width), attended, w_out), ("heads",))
    return kernel_call(last_kernel, shape(STEPS, ROWS, width), sums, output)


def solution(mesh):
    heads_size, seq_size = mesh.shape["heads"], mesh.shape["seq"]
    devices = mesh.devices.reshape(heads_size, CHIPS_Y, seq_size // CHIPS_Y // 2, 2)
    fine = Mesh(devices, ("heads", "y", "x", "core"))
    in_specs = (
        P(None, SEQ),
        P(SEQ),
        P(SEQ, "heads"),
        P(SEQ, "heads"),
        P("heads", SEQ),
        P("heads", None, SEQ, None),
        P("heads", None, SEQ, None),
        P(),
        P(),
    )
    return jax.shard_map(
        per_device, mesh=fine, in_specs=in_specs, out_specs=P(None, None, SEQ), check_vma=False
    )
```

```python
import functools
import math

import jax
import jax.numpy as jnp
from jax import lax
from jax.experimental import pallas as pl
from jax.experimental.pallas import tpu as pltpu
from jax.sharding import Mesh, PartitionSpec as P

D = 16384
STEPS = 2
EPSILON = 1e-05
ROPE_BASE = 500000.0
FILLER = -3e38
CHIPS_Y = 8
INNER = ("x", "core")
SEQ = ("y", "x", "core")

ROWS = 16
HEADS = 16
DIM = 128
GROUP = 8
OWN = ROWS // GROUP
PIECE = 40
BATCH = 2
CHUNKS = 4
SCALE = 1.0 / math.sqrt(DIM)
F32 = jnp.float32
BF16 = jnp.bfloat16


def kernel_call(body, out_shapes, *args, scratch=(), space=pltpu.VMEM, after=()):
    count = len(args)
    if after:
        inner, args = body, args + tuple(after)

        def body(*refs):
            inner(*refs[:count], *refs[len(args) :])

    single = not isinstance(out_shapes, (list, tuple))
    vmem = pl.BlockSpec(memory_space=pltpu.VMEM)
    return pl.pallas_call(
        body,
        out_shape=out_shapes,
        in_specs=[pl.BlockSpec(memory_space=space)] * len(args),
        out_specs=vmem if single else [vmem] * len(out_shapes),
        scratch_shapes=list(scratch),
        compiler_params=pltpu.CompilerParams(vmem_limit_bytes=16 * 1024 * 1024),
    )(*args)


def shape(*dims):
    return jax.ShapeDtypeStruct(dims, F32)


def core_row(i, core):
    return i // OWN * (2 * OWN) + core * OWN + i % OWN


def project(wide, gain_ref, wq_ref, wkv_ref, pieces_ref, waits=None):
    gained = (wide * gain_ref[0:1, :]).astype(BF16)

    def put(row, block):
        for r in range(OWN):
            pieces_ref[pl.ds(row(r), GROUP, stride=PIECE), :] = block[r * GROUP : (r + 1) * GROUP]

    for j in range(HEADS // 2):
        if waits:
            waits[j]()
        both = jnp.dot(gained, wq_ref[:, 2 * j * DIM : 2 * (j + 1) * DIM], preferred_element_type=F32)
        for k in range(2):
            put(lambda r: r * HEADS + 2 * j + k, both[:, k * DIM : (k + 1) * DIM])
    if waits:
        waits[-1]()
    both = jnp.dot(gained, wkv_ref[...], preferred_element_type=F32)
    put(lambda r: 2 * HEADS + r, both[:, :DIM])
    put(lambda r: 2 * HEADS + OWN + r, both[:, DIM:])
    squares = jnp.broadcast_to(jnp.sum(wide * wide, axis=1, keepdims=True), (ROWS, DIM))
    put(lambda r: 2 * HEADS + 2 * OWN + r, squares)
    put(lambda r: 2 * HEADS + 3 * OWN + r, jnp.zeros((ROWS, DIM), F32))


def first_kernel(
    tokens_hbm, gain_hbm, wq_hbm, wkv_hbm, lengths_hbm, positions_hbm,
    pieces_ref, wide_ref, gain_ref, seen_ref, *refs,
):
    table_refs, (tokens_ref, gain_in, wq_ref, wkv_ref, lengths_ref, positions_ref, left_ref, right_ref, sems) = (
        refs[:STEPS], refs[STEPS:],
    )
    chunk = wq_ref.shape[1] // CHUNKS
    pairs = [
        (lengths_hbm, lengths_ref),
        (positions_hbm, positions_ref),
        (tokens_hbm, tokens_ref),
        (gain_hbm, gain_in),
        (wkv_hbm, wkv_ref),
    ]
    columns = [pl.ds(c * chunk, chunk) for c in range(CHUNKS)]
    pairs += [(wq_hbm.at[:, c], wq_ref.at[:, c]) for c in columns]
    copies = [pltpu.make_async_copy(a, b, sems.at[i]) for i, (a, b) in enumerate(pairs)]
    for copy in copies:
        copy.start()
    inner = lax.axis_index("x") * 2 + lax.axis_index("core")
    core = lax.axis_index("core")
    seq_here = seen_ref.shape[1] // 2
    column = lax.broadcasted_iota(jnp.int32, (1, 2 * seq_here), 1)
    block = lax.axis_index("y") * GROUP + lax.axis_index("x") * 2
    spot = jnp.where(
        column < seq_here, (block + core) * seq_here + column, (block - core) * seq_here + column
    )
    copies[0].wait()
    copies[1].wait()
    for i in range(ROWS // 2):
        seen_ref[i : i + 1, :] = jnp.where(spot < lengths_ref[core_row(i, core)], 1.0, 0.0)
    lane = lax.broadcasted_iota(jnp.int32, (8, DIM), 1)
    line = lax.broadcasted_iota(jnp.int32, (8, DIM), 0)
    index = jnp.where(lane < DIM // 2, lane, lane - DIM // 2).astype(F32)
    freqs = jnp.exp(index * (-2.0 * math.log(ROPE_BASE) / DIM))
    place = jnp.where(line % 2 == 1, positions_ref[inner * OWN + 1], positions_ref[inner * OWN])
    for step, ref in enumerate(table_refs):
        angles = (place + step).astype(F32) * freqs
        sine = jnp.sin(angles)
        ref[...] = jnp.where(line < OWN, jnp.cos(angles), jnp.where(lane < DIM // 2, -sine, sine))
    copies[2].wait()
    copies[3].wait()
    width = tokens_ref.shape[1] // 2
    left_ref[...] = tokens_ref[:, :width].astype(F32)
    right_ref[...] = tokens_ref[:, width:].astype(F32)
    wide = jnp.concatenate(
        [
            jnp.concatenate([ref[pl.ds(r, GROUP, stride=OWN), :] for r in range(OWN)], axis=0)
            for ref in (left_ref, right_ref)
        ],
        axis=1,
    )
    wide_ref[...] = wide
    gain_ref[...] = jnp.broadcast_to(gain_in[...].astype(F32).reshape(1, 2 * width), gain_ref.shape)
    waits = [lambda j=j: copies[5 + j * 2 * DIM // chunk].wait() if j * 2 * DIM % chunk == 0 else None for j in range(HEADS // 2)]
    project(wide, gain_ref, wq_ref, wkv_ref, pieces_ref, waits + [copies[4].wait])


def next_kernel(sums_ref, last_ref, gain_ref, wq_ref, wkv_ref, pieces_ref, output_ref):
    output = sums_ref[0]
    for s in range(1, GROUP):
        output = output + sums_ref[s]
    output_ref[...] = output
    wide = (last_ref[...] + output).astype(BF16).astype(F32)
    project(wide, gain_ref, wq_ref, wkv_ref, pieces_ref)


def last_kernel(sums_ref, first_ref, result_ref):
    output = sums_ref[0]
    for s in range(1, GROUP):
        output = output + sums_ref[s]
    for step, value in enumerate((first_ref[...], output)):
        for b in range(ROWS):
            at = b % OWN * GROUP + b // OWN
            result_ref[step, b : b + 1, :] = value[at : at + 1, :]


def turn_kernel(parts_ref, table_ref, pieces_ref, own_ref):
    whole = parts_ref[0]
    for s in range(1, GROUP):
        whole = whole + parts_ref[s]
    table = table_ref[...]
    below = whole[2 * HEADS :]
    first = 2 * OWN
    inverse = [lax.rsqrt(below[first + r : first + r + 1] / D + EPSILON) for r in range(OWN)]
    cosine = [table[r : r + 1] for r in range(OWN)]
    sine = [table[OWN + r : OWN + r + 1] for r in range(OWN)]
    blocks = []
    for r in range(OWN):
        scaled = whole[r * HEADS : (r + 1) * HEADS] * inverse[r]
        blocks.append(scaled * cosine[r] + pltpu.roll(scaled, DIM // 2, 1) * sine[r])
    line = lax.broadcasted_iota(jnp.int32, below.shape, 0)
    odd = line % 2 == 1
    scaled = below * jnp.where(odd, inverse[1], inverse[0])
    cosines = jnp.where(line < OWN, jnp.where(odd, cosine[1], cosine[0]), 1.0)
    sines = jnp.where(line < OWN, jnp.where(odd, sine[1], sine[0]), 0.0)
    blocks.append(scaled * cosines + pltpu.roll(scaled, DIM // 2, 1) * sines)
    piece = jnp.concatenate(blocks, axis=0)
    own_ref[...] = piece
    for d in range(pieces_ref.shape[0]):
        pieces_ref[d] = piece[: 2 * HEADS]


def diagonal():
    shape_here = (2 * HEADS, DIM)
    return lax.broadcasted_iota(jnp.int32, shape_here, 0) == lax.broadcasted_iota(jnp.int32, shape_here, 1)


def to_lanes(column):
    return jnp.sum(jnp.where(diagonal(), column, 0.0), axis=0, keepdims=True)


def to_column(line):
    return jnp.sum(jnp.where(diagonal(), line, 0.0), axis=1, keepdims=True)


def stats_block(top, total):
    line = lax.broadcasted_iota(jnp.int32, (PIECE - 2 * HEADS, DIM), 0)
    return jnp.where(line == 0, top, jnp.where(line == 1, total, 0.0))


def swap_kernel(keys_ref, values_ref, other_ref):
    core = lax.axis_index("core")
    for i in range(ROWS // 2):
        b = core_row(i, 1 - core)
        other_ref[0, i] = keys_ref[b].astype(F32)
        other_ref[1, i] = values_ref[b].astype(F32)


def attend_kernel(queries_ref, keys_ref, values_ref, other_ref, seen_ref, pieces_ref, work_ref):
    core = lax.axis_index("core")
    seq_here = keys_ref.shape[1]
    halves = (slice(0, seq_here), slice(seq_here, 2 * seq_here))

    def place(i):
        return i // OWN, slice(i % OWN * HEADS, (i % OWN + 1) * HEADS)

    for i in range(ROWS // 2):
        x, heads = place(i)
        queries = queries_ref[x, heads, :].astype(BF16)
        for half, keys in zip(halves, (keys_ref[core_row(i, core)], other_ref[0, i].astype(BF16))):
            work_ref[i, :, half] = lax.dot_general(
                queries, keys, (((1,), (1,)), ((), ())), preferred_element_type=F32
            )
    for c in range(0, ROWS // 2, BATCH):
        scores = work_ref[c : c + BATCH] * SCALE
        seen = jnp.broadcast_to(seen_ref[c : c + BATCH, :][:, None, :], scores.shape) > 0.0
        tops = jnp.max(jnp.where(seen, scores, FILLER), axis=2, keepdims=True)
        probs = jnp.where(seen, jnp.exp(scores - tops), 0.0)
        totals = jnp.sum(probs, axis=2, keepdims=True)
        work_ref[c : c + BATCH] = probs
        for b in range(0, BATCH, OWN):
            top = tops[b : b + OWN].reshape(OWN * HEADS, 1)
            total = totals[b : b + OWN].reshape(OWN * HEADS, 1)
            pieces_ref[(c + b) // OWN, 2 * HEADS :, :] = stats_block(to_lanes(top), to_lanes(total))
    for i in range(ROWS // 2):
        x, heads = place(i)
        own, other = (work_ref[i, :, half].astype(BF16) for half in halves)
        pieces_ref[x, heads, :] = jnp.dot(
            own, values_ref[core_row(i, core)], preferred_element_type=F32
        ) + jnp.dot(other, other_ref[1, i].astype(BF16), preferred_element_type=F32)


def merge(parts_ref):
    tops = [parts_ref[s, 2 * HEADS : 2 * HEADS + 1, :] for s in range(parts_ref.shape[0])]
    top = functools.reduce(jnp.maximum, tops)
    total, weighted = None, None
    for s in range(parts_ref.shape[0]):
        factor = jnp.exp(tops[s] - top)
        here = factor * parts_ref[s, 2 * HEADS + 1 : 2 * HEADS + 2, :]
        part = to_column(factor) * parts_ref[s, : 2 * HEADS, :]
        total = here if total is None else total + here
        weighted = part if weighted is None else weighted + part
    return top, total, weighted


def merge_kernel(parts_ref, pieces_ref):
    top, total, weighted = merge(parts_ref)
    stats = stats_block(top, total)
    for d in range(GROUP):
        pieces_ref[d, : 2 * HEADS, :] = weighted
        pieces_ref[d, 2 * HEADS :, :] = stats


def finish_kernel(parts_ref, *refs):
    own_refs, pieces_ref = refs[:-1], refs[-1]

    def rounded(value):
        return value.astype(BF16).astype(F32)

    def spread(ref, line):
        return jnp.concatenate(
            [jnp.broadcast_to(rounded(ref[line + r : line + r + 1, :]), (HEADS, DIM)) for r in range(OWN)], axis=0
        )

    top, total, weighted = merge(parts_ref)
    top, total = to_column(top), to_column(total)
    queries = rounded(own_refs[-1][: 2 * HEADS, :])
    scores = [jnp.sum(queries * spread(ref, 2 * HEADS), axis=1, keepdims=True) * SCALE for ref in own_refs]
    whole_top = functools.reduce(jnp.maximum, scores, top)
    factor = jnp.exp(top - whole_top)
    total = total * factor
    weighted = weighted * factor
    for score, ref in zip(scores, own_refs):
        prob = jnp.exp(score - whole_top)
        total = total + prob
        weighted = weighted + rounded(prob) * spread(ref, 2 * HEADS + OWN)
    attended = weighted / total
    for d in range(GROUP):
        pieces_ref[d] = attended


def out_kernel(attended_ref, wout_ref, pieces_ref):
    partial = None
    for j in range(HEADS // 2):
        heads = jnp.concatenate(
            [
                jnp.concatenate(
                    [attended_ref[pl.ds(r * HEADS + 2 * j + k, GROUP, stride=2 * HEADS), :] for r in range(OWN)], axis=0
                )
                for k in range(2)
            ],
            axis=1,
        ).astype(BF16)
        term = jnp.dot(heads, wout_ref[2 * j * DIM : 2 * (j + 1) * DIM, :], preferred_element_type=F32)
        partial = term if partial is None else partial + term
    for d in range(GROUP):
        pieces_ref[d] = partial


def exchange(pieces, axes):
    return lax.all_to_all(pieces, axes, 0, 0, tiled=True)


def per_device(tokens, norm_gain, w_query, w_kv, w_out, key_cache, value_cache, lengths, positions):
    seq_here = key_cache.shape[2]
    width = tokens.shape[1]
    keys, values = key_cache[0], value_cache[0]
    flat = shape(GROUP * PIECE, DIM)
    cube = shape(GROUP, PIECE, DIM)
    half = pltpu.VMEM((ROWS, width // 2), F32)
    work = pltpu.VMEM((ROWS // 2, HEADS, 2 * seq_here), F32)
    line = shape(8, DIM)
    pieces, wide, gain, seen, *tables = kernel_call(
        first_kernel,
        [flat, shape(ROWS, width), shape(8, width), shape(ROWS // 2, 2 * seq_here)] + [line] * STEPS,
        *[
            pltpu.with_memory_space_constraint(array, pltpu.HBM)
            for array in (tokens, norm_gain, w_query, w_kv, lengths, positions)
        ],
        scratch=[
            pltpu.VMEM(tokens.shape, BF16),
            pltpu.VMEM(norm_gain.shape, BF16),
            pltpu.VMEM(w_query.shape, BF16),
            pltpu.VMEM(w_kv.shape, BF16),
            pltpu.SMEM(lengths.shape, jnp.int32),
            pltpu.SMEM(positions.shape, jnp.int32),
            half,
            half,
            pltpu.SemaphoreType.DMA((5 + CHUNKS,)),
        ],
        space=pltpu.HBM,
    )
    own, output = [], None
    for step in range(STEPS):
        if step:
            pieces, output = kernel_call(
                next_kernel, [flat, shape(ROWS, width)], sums, wide, gain, w_query, w_kv, after=(other,)
            )
        parts = exchange(pieces.reshape(GROUP, PIECE, DIM), INNER)
        total = jnp.broadcast_to(jnp.sum(parts, axis=0)[None], (GROUP, PIECE, DIM))
        parts = exchange(total, ("y",))
        if not step:
            other = kernel_call(swap_kernel, shape(2, ROWS // 2, seq_here, DIM), keys, values, after=(parts,))
            parts, other = lax.optimization_barrier((parts, other))
            other = lax.ppermute(other, "core", [(0, 1), (1, 0)])
        pieces, mine = kernel_call(turn_kernel, [shape(GROUP // 2, 2 * HEADS, DIM), shape(PIECE, DIM)], parts, tables[step], after=(other,) if step else ())
        own.append(mine)
        queries = exchange(pieces, ("x",))
        pieces = kernel_call(
            attend_kernel, shape(GROUP // 2, PIECE, DIM), queries, keys, values, other, seen, scratch=[work]
        )
        parts = exchange(pieces, ("x",))
        kept = () if step else (other,)
        parts = exchange(kernel_call(merge_kernel, cube, parts, after=kept), ("y",))
        pieces = kernel_call(finish_kernel, shape(GROUP, 2 * HEADS, DIM), parts, *own, after=kept)
        attended = exchange(pieces, INNER).reshape(GROUP * 2 * HEADS, DIM)
        sums = exchange(kernel_call(out_kernel, shape(GROUP, ROWS, width), attended, w_out, after=kept), ("heads",))
    return kernel_call(last_kernel, shape(STEPS, ROWS, width), sums, output)


def solution(mesh):
    heads_size, seq_size = mesh.shape["heads"], mesh.shape["seq"]
    devices = mesh.devices.reshape(heads_size, CHIPS_Y, seq_size // CHIPS_Y // 2, 2)
    fine = Mesh(devices, ("heads", "y", "x", "core"))
    in_specs = (
        P(None, SEQ),
        P(SEQ),
        P(SEQ, "heads"),
        P(SEQ, "heads"),
        P("heads", SEQ),
        P("heads", None, SEQ, None),
        P("heads", None, SEQ, None),
        P(),
        P(),
    )
    return jax.shard_map(
        per_device, mesh=fine, in_specs=in_specs, out_specs=P(None, None, SEQ), check_vma=False
    )
```

```python
import functools
import math

import jax
import jax.numpy as jnp
from jax import lax
from jax.experimental import pallas as pl
from jax.experimental.pallas import tpu as pltpu
from jax.sharding import Mesh, PartitionSpec as P

D = 16384
STEPS = 2
EPSILON = 1e-05
ROPE_BASE = 500000.0
FILLER = -3e38
CHIPS_Y = 8
INNER = ("x", "core")
SEQ = ("y", "x", "core")

ROWS = 16
HEADS = 16
DIM = 128
GROUP = 8
OWN = ROWS // GROUP
PIECE = 40
BATCH = 2
CHUNKS = 2
DENSE = 33
SCALE = 1.0 / math.sqrt(DIM)
F32 = jnp.float32
BF16 = jnp.bfloat16


def kernel_call(body, out_shapes, *args, scratch=(), space=pltpu.VMEM, after=()):
    count = len(args)
    if after:
        inner, args = body, args + tuple(after)

        def body(*refs):
            inner(*refs[:count], *refs[len(args) :])

    single = not isinstance(out_shapes, (list, tuple))
    vmem = pl.BlockSpec(memory_space=pltpu.VMEM)
    return pl.pallas_call(
        body,
        out_shape=out_shapes,
        in_specs=[pl.BlockSpec(memory_space=space)] * len(args),
        out_specs=vmem if single else [vmem] * len(out_shapes),
        scratch_shapes=list(scratch),
        compiler_params=pltpu.CompilerParams(vmem_limit_bytes=16 * 1024 * 1024),
    )(*args)


def shape(*dims):
    return jax.ShapeDtypeStruct(dims, F32)


def core_row(i, core):
    return i // OWN * (2 * OWN) + core * OWN + i % OWN


def project(wide, gain_ref, wq_ref, wkv_ref, pieces_ref, waits=None):
    gained = (wide * gain_ref[0:1, :]).astype(BF16)

    def put(row, block):
        for r in range(OWN):
            pieces_ref[pl.ds(row(r), GROUP, stride=PIECE), :] = block[r * GROUP : (r + 1) * GROUP]

    for j in range(HEADS // 2):
        if waits:
            waits[j]()
        both = jnp.dot(gained, wq_ref[:, 2 * j * DIM : 2 * (j + 1) * DIM], preferred_element_type=F32)
        for k in range(2):
            put(lambda r: r * HEADS + 2 * j + k, both[:, k * DIM : (k + 1) * DIM])
    if waits:
        waits[-1]()
    both = jnp.dot(gained, wkv_ref[...], preferred_element_type=F32)
    put(lambda r: 2 * HEADS + r, both[:, :DIM])
    put(lambda r: 2 * HEADS + OWN + r, both[:, DIM:])
    squares = jnp.broadcast_to(jnp.sum(wide * wide, axis=1, keepdims=True), (ROWS, DIM))
    put(lambda r: 2 * HEADS + 2 * OWN + r, squares)
    put(lambda r: 2 * HEADS + 3 * OWN + r, jnp.zeros((ROWS, DIM), F32))


def first_kernel(
    tokens_hbm, gain_hbm, wq_hbm, wkv_hbm, lengths_hbm, positions_hbm,
    pieces_ref, wide_ref, gain_ref, seen_ref, *refs,
):
    table_refs, (tokens_ref, gain_in, wq_ref, wkv_ref, lengths_ref, positions_ref, left_ref, right_ref, sems) = (
        refs[:STEPS], refs[STEPS:],
    )
    chunk = wq_ref.shape[1] // CHUNKS
    pairs = [
        (lengths_hbm, lengths_ref),
        (positions_hbm, positions_ref),
        (tokens_hbm, tokens_ref),
        (gain_hbm, gain_in),
        (wkv_hbm, wkv_ref),
    ]
    columns = [pl.ds(c * chunk, chunk) for c in range(CHUNKS)]
    pairs += [(wq_hbm.at[:, c], wq_ref.at[:, c]) for c in columns]
    copies = [pltpu.make_async_copy(a, b, sems.at[i]) for i, (a, b) in enumerate(pairs)]
    for copy in copies[5:] + copies[:5]:
        copy.start()
    inner = lax.axis_index("x") * 2 + lax.axis_index("core")
    core = lax.axis_index("core")
    seq_here = seen_ref.shape[1] // 2
    column = lax.broadcasted_iota(jnp.int32, (1, 2 * seq_here), 1)
    block = lax.axis_index("y") * GROUP + lax.axis_index("x") * 2
    spot = jnp.where(
        column < seq_here, (block + core) * seq_here + column, (block - core) * seq_here + column
    )
    copies[0].wait()
    copies[1].wait()
    for i in range(ROWS // 2):
        seen_ref[i : i + 1, :] = jnp.where(spot < lengths_ref[core_row(i, core)], 1.0, 0.0)
    lane = lax.broadcasted_iota(jnp.int32, (8, DIM), 1)
    line = lax.broadcasted_iota(jnp.int32, (8, DIM), 0)
    index = jnp.where(lane < DIM // 2, lane, lane - DIM // 2).astype(F32)
    freqs = jnp.exp(index * (-2.0 * math.log(ROPE_BASE) / DIM))
    place = jnp.where(line % 2 == 1, positions_ref[inner * OWN + 1], positions_ref[inner * OWN])
    for step, ref in enumerate(table_refs):
        angles = (place + step).astype(F32) * freqs
        sine = jnp.sin(angles)
        ref[...] = jnp.where(line < OWN, jnp.cos(angles), jnp.where(lane < DIM // 2, -sine, sine))
    copies[2].wait()
    copies[3].wait()
    width = tokens_ref.shape[1] // 2
    left_ref[...] = tokens_ref[:, :width].astype(F32)
    right_ref[...] = tokens_ref[:, width:].astype(F32)
    wide = jnp.concatenate(
        [
            jnp.concatenate([ref[pl.ds(r, GROUP, stride=OWN), :] for r in range(OWN)], axis=0)
            for ref in (left_ref, right_ref)
        ],
        axis=1,
    )
    wide_ref[...] = wide
    gain_ref[...] = jnp.broadcast_to(gain_in[...].astype(F32).reshape(1, 2 * width), gain_ref.shape)
    waits = [lambda j=j: copies[5 + j * 2 * DIM // chunk].wait() if j * 2 * DIM % chunk == 0 else None for j in range(HEADS // 2)]
    project(wide, gain_ref, wq_ref, wkv_ref, pieces_ref, waits + [copies[4].wait])


def next_kernel(sums_ref, last_ref, gain_ref, wq_ref, wkv_ref, pieces_ref, output_ref):
    output = sums_ref[0]
    for s in range(1, GROUP):
        output = output + sums_ref[s]
    output_ref[...] = output
    wide = (last_ref[...] + output).astype(BF16).astype(F32)
    project(wide, gain_ref, wq_ref, wkv_ref, pieces_ref)


def last_kernel(sums_ref, first_ref, result_ref):
    output = sums_ref[0]
    for s in range(1, GROUP):
        output = output + sums_ref[s]
    for step, value in enumerate((first_ref[...], output)):
        for b in range(ROWS):
            at = b % OWN * GROUP + b // OWN
            result_ref[step, b : b + 1, :] = value[at : at + 1, :]


def turn_kernel(parts_ref, table_ref, pieces_ref, own_ref):
    whole = parts_ref[0]
    for s in range(1, GROUP):
        whole = whole + parts_ref[s]
    table = table_ref[...]
    below = whole[2 * HEADS :]
    first = 2 * OWN
    inverse = [lax.rsqrt(below[first + r : first + r + 1] / D + EPSILON) for r in range(OWN)]
    cosine = [table[r : r + 1] for r in range(OWN)]
    sine = [table[OWN + r : OWN + r + 1] for r in range(OWN)]
    blocks = []
    for r in range(OWN):
        scaled = whole[r * HEADS : (r + 1) * HEADS] * inverse[r]
        blocks.append(scaled * cosine[r] + pltpu.roll(scaled, DIM // 2, 1) * sine[r])
    line = lax.broadcasted_iota(jnp.int32, below.shape, 0)
    odd = line % 2 == 1
    scaled = below * jnp.where(odd, inverse[1], inverse[0])
    cosines = jnp.where(line < OWN, jnp.where(odd, cosine[1], cosine[0]), 1.0)
    sines = jnp.where(line < OWN, jnp.where(odd, sine[1], sine[0]), 0.0)
    blocks.append(scaled * cosines + pltpu.roll(scaled, DIM // 2, 1) * sines)
    piece = jnp.concatenate(blocks, axis=0)
    own_ref[...] = piece
    for d in range(pieces_ref.shape[0]):
        pieces_ref[d] = piece[: 2 * HEADS]


def diagonal():
    shape_here = (2 * HEADS, DIM)
    return lax.broadcasted_iota(jnp.int32, shape_here, 0) == lax.broadcasted_iota(jnp.int32, shape_here, 1)


def to_lanes(column):
    return jnp.sum(jnp.where(diagonal(), column, 0.0), axis=0, keepdims=True)


def to_column(line):
    return jnp.sum(jnp.where(diagonal(), line, 0.0), axis=1, keepdims=True)


def joined(top, total):
    lane = lax.broadcasted_iota(jnp.int32, (1, DIM), 1)
    return jnp.where(lane < 2 * HEADS, top, jnp.where(lane < 4 * HEADS, pltpu.roll(total, 2 * HEADS, 1), 0.0))


def swap_kernel(keys_ref, values_ref, other_ref):
    core = lax.axis_index("core")
    for i in range(ROWS // 2):
        b = core_row(i, 1 - core)
        other_ref[0, i] = keys_ref[b].astype(F32)
        other_ref[1, i] = values_ref[b].astype(F32)


def attend_kernel(queries_ref, keys_ref, values_ref, other_ref, seen_ref, pieces_ref, work_ref):
    core = lax.axis_index("core")
    seq_here = keys_ref.shape[1]
    halves = (slice(0, seq_here), slice(seq_here, 2 * seq_here))

    def place(i):
        return i // OWN, slice(i % OWN * HEADS, (i % OWN + 1) * HEADS)

    for i in range(ROWS // 2):
        x, heads = place(i)
        queries = queries_ref[x, heads, :].astype(BF16)
        for half, keys in zip(halves, (keys_ref[core_row(i, core)], other_ref[0, i].astype(BF16))):
            work_ref[i, :, half] = lax.dot_general(
                queries, keys, (((1,), (1,)), ((), ())), preferred_element_type=F32
            )
    for c in range(0, ROWS // 2, BATCH):
        scores = work_ref[c : c + BATCH] * SCALE
        seen = jnp.broadcast_to(seen_ref[c : c + BATCH, :][:, None, :], scores.shape) > 0.0
        tops = jnp.max(jnp.where(seen, scores, FILLER), axis=2, keepdims=True)
        probs = jnp.where(seen, jnp.exp(scores - tops), 0.0)
        totals = jnp.sum(probs, axis=2, keepdims=True)
        work_ref[c : c + BATCH] = probs
        for b in range(0, BATCH, OWN):
            top = tops[b : b + OWN].reshape(OWN * HEADS, 1)
            total = totals[b : b + OWN].reshape(OWN * HEADS, 1)
            stats = joined(to_lanes(top), to_lanes(total))
            pieces_ref[(c + b) // OWN, 2 * HEADS :, :] = jnp.broadcast_to(stats, (PIECE - 2 * HEADS, DIM))
    for i in range(ROWS // 2):
        x, heads = place(i)
        own, other = (work_ref[i, :, half].astype(BF16) for half in halves)
        pieces_ref[x, heads, :] = jnp.dot(
            own, values_ref[core_row(i, core)], preferred_element_type=F32
        ) + jnp.dot(other, other_ref[1, i].astype(BF16), preferred_element_type=F32)


def merge(weighted, stats):
    top = functools.reduce(jnp.maximum, stats)
    total, whole = None, None
    for part, stat in zip(weighted, stats):
        factor = jnp.exp(stat - top)
        here = factor * pltpu.roll(stat, DIM - 2 * HEADS, 1)
        part = to_column(factor) * part
        total = here if total is None else total + here
        whole = part if whole is None else whole + part
    return top, total, whole


def merge_kernel(parts_ref, pieces_ref):
    top, total, weighted = merge(*zip(*[
        (parts_ref[s, : 2 * HEADS, :], parts_ref[s, 2 * HEADS : 2 * HEADS + 1, :]) for s in range(parts_ref.shape[0])
    ]))
    stats = joined(top, total)
    for d in range(GROUP):
        pieces_ref[d * DENSE : d * DENSE + 2 * HEADS, :] = weighted
        pieces_ref[d * DENSE + 2 * HEADS : (d + 1) * DENSE, :] = stats


def finish_kernel(parts_ref, *refs):
    own_refs, pieces_ref = refs[:-1], refs[-1]

    def rounded(value):
        return value.astype(BF16).astype(F32)

    def spread(ref, line):
        return jnp.concatenate(
            [jnp.broadcast_to(rounded(ref[line + r : line + r + 1, :]), (HEADS, DIM)) for r in range(OWN)], axis=0
        )

    top, total, weighted = merge(*zip(*[
        (parts_ref[s * DENSE : s * DENSE + 2 * HEADS, :], parts_ref[s * DENSE + 2 * HEADS : (s + 1) * DENSE, :])
        for s in range(GROUP)
    ]))
    top, total = to_column(top), to_column(total)
    queries = rounded(own_refs[-1][: 2 * HEADS, :])
    scores = [jnp.sum(queries * spread(ref, 2 * HEADS), axis=1, keepdims=True) * SCALE for ref in own_refs]
    whole_top = functools.reduce(jnp.maximum, scores, top)
    factor = jnp.exp(top - whole_top)
    total = total * factor
    weighted = weighted * factor
    for score, ref in zip(scores, own_refs):
        prob = jnp.exp(score - whole_top)
        total = total + prob
        weighted = weighted + rounded(prob) * spread(ref, 2 * HEADS + OWN)
    attended = weighted / total
    for d in range(GROUP):
        pieces_ref[d] = attended


def out_kernel(attended_ref, wout_ref, pieces_ref):
    partial = None
    for j in range(HEADS // 2):
        heads = jnp.concatenate(
            [
                jnp.concatenate(
                    [attended_ref[pl.ds(r * HEADS + 2 * j + k, GROUP, stride=2 * HEADS), :] for r in range(OWN)], axis=0
                )
                for k in range(2)
            ],
            axis=1,
        ).astype(BF16)
        term = jnp.dot(heads, wout_ref[2 * j * DIM : 2 * (j + 1) * DIM, :], preferred_element_type=F32)
        partial = term if partial is None else partial + term
    for d in range(GROUP):
        pieces_ref[d] = partial


def exchange(pieces, axes):
    return lax.all_to_all(pieces, axes, 0, 0, tiled=True)


def per_device(tokens, norm_gain, w_query, w_kv, w_out, key_cache, value_cache, lengths, positions):
    seq_here = key_cache.shape[2]
    width = tokens.shape[1]
    keys, values = key_cache[0], value_cache[0]
    flat = shape(GROUP * PIECE, DIM)
    half = pltpu.VMEM((ROWS, width // 2), F32)
    work = pltpu.VMEM((ROWS // 2, HEADS, 2 * seq_here), F32)
    line = shape(8, DIM)
    pieces, wide, gain, seen, *tables = kernel_call(
        first_kernel,
        [flat, shape(ROWS, width), shape(8, width), shape(ROWS // 2, 2 * seq_here)] + [line] * STEPS,
        *[
            pltpu.with_memory_space_constraint(array, pltpu.HBM)
            for array in (tokens, norm_gain, w_query, w_kv, lengths, positions)
        ],
        scratch=[
            pltpu.VMEM(tokens.shape, BF16),
            pltpu.VMEM(norm_gain.shape, BF16),
            pltpu.VMEM(w_query.shape, BF16),
            pltpu.VMEM(w_kv.shape, BF16),
            pltpu.SMEM(lengths.shape, jnp.int32),
            pltpu.SMEM(positions.shape, jnp.int32),
            half,
            half,
            pltpu.SemaphoreType.DMA((5 + CHUNKS,)),
        ],
        space=pltpu.HBM,
    )
    own, output = [], None
    for step in range(STEPS):
        if step:
            pieces, output = kernel_call(
                next_kernel, [flat, shape(ROWS, width)], sums, wide, gain, w_query, w_kv, after=(other,)
            )
        parts = exchange(pieces.reshape(GROUP, PIECE, DIM), INNER)
        total = jnp.broadcast_to(jnp.sum(parts, axis=0)[None], (GROUP, PIECE, DIM))
        parts = exchange(total, ("y",))
        if not step:
            other = kernel_call(swap_kernel, shape(2, ROWS // 2, seq_here, DIM), keys, values, after=(parts,))
            parts, other = lax.optimization_barrier((parts, other))
            other = lax.ppermute(other, "core", [(0, 1), (1, 0)])
        pieces, mine = kernel_call(turn_kernel, [shape(GROUP // 2, 2 * HEADS, DIM), shape(PIECE, DIM)], parts, tables[step], after=(other,) if step else ())
        own.append(mine)
        queries = exchange(pieces, ("x",))
        pieces = kernel_call(
            attend_kernel, shape(GROUP // 2, PIECE, DIM), queries, keys, values, other, seen, scratch=[work]
        )
        parts = exchange(pieces, ("x",))
        kept = () if step else (other,)
        pieces = kernel_call(merge_kernel, shape(GROUP * DENSE, DIM), parts, after=kept)
        parts = exchange(pieces.reshape(GROUP, 1, DENSE * DIM), ("y",)).reshape(GROUP * DENSE, DIM)
        pieces = kernel_call(finish_kernel, shape(GROUP, 2 * HEADS, DIM), parts, *own, after=kept)
        attended = exchange(pieces, INNER).reshape(GROUP * 2 * HEADS, DIM)
        sums = exchange(kernel_call(out_kernel, shape(GROUP, ROWS, width), attended, w_out, after=kept), ("heads",))
    return kernel_call(last_kernel, shape(STEPS, ROWS, width), sums, output)


def solution(mesh):
    heads_size, seq_size = mesh.shape["heads"], mesh.shape["seq"]
    devices = mesh.devices.reshape(heads_size, CHIPS_Y, seq_size // CHIPS_Y // 2, 2)
    fine = Mesh(devices, ("heads", "y", "x", "core"))
    in_specs = (
        P(None, SEQ),
        P(SEQ),
        P(SEQ, "heads"),
        P(SEQ, "heads"),
        P("heads", SEQ),
        P("heads", None, SEQ, None),
        P("heads", None, SEQ, None),
        P(),
        P(),
    )
    return jax.shard_map(
        per_device, mesh=fine, in_specs=in_specs, out_specs=P(None, None, SEQ), check_vma=False
    )
```

```python
import functools
import math

import jax
import jax.numpy as jnp
from jax import lax
from jax.experimental import pallas as pl
from jax.experimental.pallas import tpu as pltpu
from jax.sharding import Mesh, PartitionSpec as P

D = 16384
STEPS = 2
EPSILON = 1e-05
ROPE_BASE = 500000.0
FILLER = -3e38
CHIPS_Y = 8
INNER = ("x", "core")
SEQ = ("y", "x", "core")

ROWS = 16
HEADS = 16
DIM = 128
GROUP = 8
OWN = ROWS // GROUP
PIECE = 40
BATCH = 2
CHUNKS = 2
DENSE = 33
SHARE = 5
QUARTER = HEADS // 4
SCALE = 1.0 / math.sqrt(DIM)
F32 = jnp.float32
BF16 = jnp.bfloat16


def kernel_call(body, out_shapes, *args, scratch=(), space=pltpu.VMEM, after=()):
    count = len(args)
    if after:
        inner, args = body, args + tuple(after)

        def body(*refs):
            inner(*refs[:count], *refs[len(args) :])

    single = not isinstance(out_shapes, (list, tuple))
    vmem = pl.BlockSpec(memory_space=pltpu.VMEM)
    return pl.pallas_call(
        body,
        out_shape=out_shapes,
        in_specs=[pl.BlockSpec(memory_space=space)] * len(args),
        out_specs=vmem if single else [vmem] * len(out_shapes),
        scratch_shapes=list(scratch),
        compiler_params=pltpu.CompilerParams(vmem_limit_bytes=16 * 1024 * 1024),
    )(*args)


def shape(*dims):
    return jax.ShapeDtypeStruct(dims, F32)


def core_row(i, core):
    return i // OWN * (2 * OWN) + core * OWN + i % OWN


def project(wide, gain_ref, wq_ref, wkv_ref, pieces_ref, waits=None, shares=False):
    gained = (wide * gain_ref[0:1, :]).astype(BF16)

    def put(head, block):
        for r in range(OWN):
            if not shares:
                start = r * HEADS + head if head < HEADS else 2 * HEADS + (head - HEADS) * OWN + r
            elif head < HEADS:
                start = (r * 4 + head // QUARTER) * GROUP * SHARE + head % QUARTER
            else:
                start = (r * 4 + head - HEADS) * GROUP * SHARE + SHARE - 1
            stride = SHARE if shares else PIECE
            pieces_ref[pl.ds(start, GROUP, stride=stride), :] = block[r * GROUP : (r + 1) * GROUP]

    for j in range(HEADS // 2):
        if waits:
            waits[j]()
        both = jnp.dot(gained, wq_ref[:, 2 * j * DIM : 2 * (j + 1) * DIM], preferred_element_type=F32)
        for k in range(2):
            put(2 * j + k, both[:, k * DIM : (k + 1) * DIM])
    if waits:
        waits[-1]()
    both = jnp.dot(gained, wkv_ref[...], preferred_element_type=F32)
    put(HEADS + 0, both[:, :DIM])
    put(HEADS + 1, both[:, DIM:])
    squares = jnp.broadcast_to(jnp.sum(wide * wide, axis=1, keepdims=True), (ROWS, DIM))
    put(HEADS + 2, squares)
    put(HEADS + 3, jnp.zeros((ROWS, DIM), F32))


def first_kernel(
    tokens_hbm, gain_hbm, wq_hbm, wkv_hbm, lengths_hbm, positions_hbm,
    pieces_ref, wide_ref, gain_ref, seen_ref, *refs,
):
    table_refs, (tokens_ref, gain_in, wq_ref, wkv_ref, lengths_ref, positions_ref, left_ref, right_ref, sems) = (
        refs[:STEPS], refs[STEPS:],
    )
    chunk = wq_ref.shape[1] // CHUNKS
    pairs = [
        (lengths_hbm, lengths_ref),
        (positions_hbm, positions_ref),
        (tokens_hbm, tokens_ref),
        (gain_hbm, gain_in),
        (wkv_hbm, wkv_ref),
    ]
    columns = [pl.ds(c * chunk, chunk) for c in range(CHUNKS)]
    pairs += [(wq_hbm.at[:, c], wq_ref.at[:, c]) for c in columns]
    copies = [pltpu.make_async_copy(a, b, sems.at[i]) for i, (a, b) in enumerate(pairs)]
    for copy in copies[5:] + copies[:5]:
        copy.start()
    inner = lax.axis_index("x") * 2 + lax.axis_index("core")
    core = lax.axis_index("core")
    seq_here = seen_ref.shape[1] // 2
    column = lax.broadcasted_iota(jnp.int32, (1, 2 * seq_here), 1)
    block = lax.axis_index("y") * GROUP + lax.axis_index("x") * 2
    spot = jnp.where(
        column < seq_here, (block + core) * seq_here + column, (block - core) * seq_here + column
    )
    copies[0].wait()
    copies[1].wait()
    for i in range(ROWS // 2):
        seen_ref[i : i + 1, :] = jnp.where(spot < lengths_ref[core_row(i, core)], 1.0, 0.0)
    lane = lax.broadcasted_iota(jnp.int32, (8, DIM), 1)
    line = lax.broadcasted_iota(jnp.int32, (8, DIM), 0)
    index = jnp.where(lane < DIM // 2, lane, lane - DIM // 2).astype(F32)
    freqs = jnp.exp(index * (-2.0 * math.log(ROPE_BASE) / DIM))
    both = (positions_ref[inner * OWN], positions_ref[inner * OWN + 1])
    one = jnp.where(lax.axis_index("y") >= 4, both[1], both[0])
    for step, ref in enumerate(table_refs):
        place = jnp.where(line % 2 == 1, both[1], both[0]) if step == 0 else jnp.broadcast_to(one, line.shape)
        angles = (place + step).astype(F32) * freqs
        sine = jnp.sin(angles)
        cosines = line < OWN if step == 0 else line == 0
        ref[...] = jnp.where(cosines, jnp.cos(angles), jnp.where(lane < DIM // 2, -sine, sine))
    copies[2].wait()
    copies[3].wait()
    width = tokens_ref.shape[1] // 2
    left_ref[...] = tokens_ref[:, :width].astype(F32)
    right_ref[...] = tokens_ref[:, width:].astype(F32)
    wide = jnp.concatenate(
        [
            jnp.concatenate([ref[pl.ds(r, GROUP, stride=OWN), :] for r in range(OWN)], axis=0)
            for ref in (left_ref, right_ref)
        ],
        axis=1,
    )
    wide_ref[...] = wide
    gain_ref[...] = jnp.broadcast_to(gain_in[...].astype(F32).reshape(1, 2 * width), gain_ref.shape)
    waits = [lambda j=j: copies[5 + j * 2 * DIM // chunk].wait() if j * 2 * DIM % chunk == 0 else None for j in range(HEADS // 2)]
    project(wide, gain_ref, wq_ref, wkv_ref, pieces_ref, waits + [copies[4].wait])


def next_kernel(sums_ref, last_ref, gain_ref, wq_ref, wkv_ref, pieces_ref, output_ref):
    output = sums_ref[0]
    for s in range(1, GROUP):
        output = output + sums_ref[s]
    output_ref[...] = output
    wide = (last_ref[...] + output).astype(BF16).astype(F32)
    project(wide, gain_ref, wq_ref, wkv_ref, pieces_ref, shares=True)


def last_kernel(sums_ref, first_ref, result_ref):
    output = sums_ref[0]
    for s in range(1, GROUP):
        output = output + sums_ref[s]
    for step, value in enumerate((first_ref[...], output)):
        for b in range(ROWS):
            at = b % OWN * GROUP + b // OWN
            result_ref[step, b : b + 1, :] = value[at : at + 1, :]


def turn_kernel(parts_ref, table_ref, pieces_ref, own_ref):
    whole = parts_ref[0]
    for s in range(1, GROUP):
        whole = whole + parts_ref[s]
    table = table_ref[...]
    below = whole[2 * HEADS :]
    first = 2 * OWN
    inverse = [lax.rsqrt(below[first + r : first + r + 1] / D + EPSILON) for r in range(OWN)]
    cosine = [table[r : r + 1] for r in range(OWN)]
    sine = [table[OWN + r : OWN + r + 1] for r in range(OWN)]
    blocks = []
    for r in range(OWN):
        scaled = whole[r * HEADS : (r + 1) * HEADS] * inverse[r]
        blocks.append(scaled * cosine[r] + pltpu.roll(scaled, DIM // 2, 1) * sine[r])
    line = lax.broadcasted_iota(jnp.int32, below.shape, 0)
    odd = line % 2 == 1
    scaled = below * jnp.where(odd, inverse[1], inverse[0])
    cosines = jnp.where(line < OWN, jnp.where(odd, cosine[1], cosine[0]), 1.0)
    sines = jnp.where(line < OWN, jnp.where(odd, sine[1], sine[0]), 0.0)
    blocks.append(scaled * cosines + pltpu.roll(scaled, DIM // 2, 1) * sines)
    piece = jnp.concatenate(blocks, axis=0)
    own_ref[0] = piece
    for d in range(pieces_ref.shape[0]):
        pieces_ref[d] = piece[: 2 * HEADS]


def turn_shares_kernel(parts_ref, table_ref, pieces_ref):
    step = GROUP * SHARE
    sums = []
    for t in range(SHARE):
        total = parts_ref[pl.ds(t, GROUP, stride=SHARE), :]
        for k in range(step, parts_ref.shape[0], step):
            total = total + parts_ref[pl.ds(k + t, GROUP, stride=SHARE), :]
        sums.append(jnp.sum(total, axis=0, keepdims=True))
    whole = jnp.concatenate(sums, axis=0)
    turned = whole * table_ref[0:1, :] + pltpu.roll(whole, DIM // 2, 1) * table_ref[1:2, :]
    line = lax.broadcasted_iota(jnp.int32, whole.shape, 0)
    quarter = jnp.broadcast_to(lax.rem(lax.axis_index("y"), 4), whole.shape)
    piece = jnp.where((line < SHARE - 1) | (quarter == 0), turned, whole)
    copies = jnp.concatenate([piece] * GROUP, axis=0)
    for k in range(0, pieces_ref.shape[0], step):
        pieces_ref[k : k + step, :] = copies


def diagonal():
    shape_here = (2 * HEADS, DIM)
    return lax.broadcasted_iota(jnp.int32, shape_here, 0) == lax.broadcasted_iota(jnp.int32, shape_here, 1)


def to_lanes(column):
    return jnp.sum(jnp.where(diagonal(), column, 0.0), axis=0, keepdims=True)


def to_column(line):
    return jnp.sum(jnp.where(diagonal(), line, 0.0), axis=1, keepdims=True)


def joined(top, total):
    lane = lax.broadcasted_iota(jnp.int32, (1, DIM), 1)
    return jnp.where(lane < 2 * HEADS, top, jnp.where(lane < 4 * HEADS, pltpu.roll(total, 2 * HEADS, 1), 0.0))


def swap_kernel(keys_ref, values_ref, other_ref):
    core = lax.axis_index("core")
    for i in range(ROWS // 2):
        b = core_row(i, 1 - core)
        other_ref[0, i] = keys_ref[b].astype(F32)
        other_ref[1, i] = values_ref[b].astype(F32)


def attend_kernel(queries_ref, keys_ref, values_ref, other_ref, seen_ref, pieces_ref, *refs):
    own_ref, work_ref = (None, *refs)[-2:]
    core = lax.axis_index("core")
    seq_here = keys_ref.shape[1]
    halves = (slice(0, seq_here), slice(seq_here, 2 * seq_here))

    def place(i):
        return i // OWN, slice(i % OWN * HEADS, (i % OWN + 1) * HEADS)

    for i in range(ROWS // 2):
        x, heads = place(i)
        if own_ref is None:
            scaled = queries_ref[x, heads, :]
        else:
            starts = [((i % OWN * 4 + quarter) * (GROUP // 2) + x) * SHARE for quarter in range(4)]
            ends = [queries_ref[start + SHARE - 1 : start + SHARE, :] for start in starts]
            inverse = lax.rsqrt(ends[2] / D + EPSILON)
            scaled = jnp.concatenate([queries_ref[start : start + QUARTER, :] for start in starts], axis=0) * inverse
            own_ref[x, heads, :] = scaled
            for k in range(2):
                line = 2 * HEADS + k * OWN + i % OWN
                own_ref[x, line : line + 1, :] = ends[k] * inverse
        queries = scaled.astype(BF16)
        for half, keys in zip(halves, (keys_ref[core_row(i, core)], other_ref[0, i].astype(BF16))):
            work_ref[i, :, half] = lax.dot_general(
                queries, keys, (((1,), (1,)), ((), ())), preferred_element_type=F32
            )
    for c in range(0, ROWS // 2, BATCH):
        scores = work_ref[c : c + BATCH] * SCALE
        seen = jnp.broadcast_to(seen_ref[c : c + BATCH, :][:, None, :], scores.shape) > 0.0
        tops = jnp.max(jnp.where(seen, scores, FILLER), axis=2, keepdims=True)
        probs = jnp.where(seen, jnp.exp(scores - tops), 0.0)
        totals = jnp.sum(probs, axis=2, keepdims=True)
        work_ref[c : c + BATCH] = probs
        for b in range(0, BATCH, OWN):
            top = tops[b : b + OWN].reshape(OWN * HEADS, 1)
            total = totals[b : b + OWN].reshape(OWN * HEADS, 1)
            stats = joined(to_lanes(top), to_lanes(total))
            pieces_ref[(c + b) // OWN, 2 * HEADS :, :] = jnp.broadcast_to(stats, (PIECE - 2 * HEADS, DIM))
    for i in range(ROWS // 2):
        x, heads = place(i)
        own, other = (work_ref[i, :, half].astype(BF16) for half in halves)
        pieces_ref[x, heads, :] = jnp.dot(
            own, values_ref[core_row(i, core)], preferred_element_type=F32
        ) + jnp.dot(other, other_ref[1, i].astype(BF16), preferred_element_type=F32)


def merge(weighted, stats):
    top = functools.reduce(jnp.maximum, stats)
    total, whole = None, None
    for part, stat in zip(weighted, stats):
        factor = jnp.exp(stat - top)
        here = factor * pltpu.roll(stat, DIM - 2 * HEADS, 1)
        part = to_column(factor) * part
        total = here if total is None else total + here
        whole = part if whole is None else whole + part
    return top, total, whole


def merge_kernel(parts_ref, pieces_ref):
    top, total, weighted = merge(*zip(*[
        (parts_ref[s, : 2 * HEADS, :], parts_ref[s, 2 * HEADS : 2 * HEADS + 1, :]) for s in range(parts_ref.shape[0])
    ]))
    stats = joined(top, total)
    for d in range(GROUP):
        pieces_ref[d * DENSE : d * DENSE + 2 * HEADS, :] = weighted
        pieces_ref[d * DENSE + 2 * HEADS : (d + 1) * DENSE, :] = stats


def finish_kernel(parts_ref, *refs):
    own_refs, pieces_ref = refs[:-1], refs[-1]
    x = lax.axis_index("x")

    def rounded(value):
        return value.astype(BF16).astype(F32)

    def spread(ref, line):
        return jnp.concatenate(
            [jnp.broadcast_to(rounded(ref[x if ref.shape[0] > 1 else 0, line + r : line + r + 1, :]), (HEADS, DIM)) for r in range(OWN)], axis=0
        )

    top, total, weighted = merge(*zip(*[
        (parts_ref[s * DENSE : s * DENSE + 2 * HEADS, :], parts_ref[s * DENSE + 2 * HEADS : (s + 1) * DENSE, :])
        for s in range(GROUP)
    ]))
    top, total = to_column(top), to_column(total)
    queries = rounded(own_refs[-1][x if own_refs[-1].shape[0] > 1 else 0, : 2 * HEADS, :])
    scores = [jnp.sum(queries * spread(ref, 2 * HEADS), axis=1, keepdims=True) * SCALE for ref in own_refs]
    whole_top = functools.reduce(jnp.maximum, scores, top)
    factor = jnp.exp(top - whole_top)
    total = total * factor
    weighted = weighted * factor
    for score, ref in zip(scores, own_refs):
        prob = jnp.exp(score - whole_top)
        total = total + prob
        weighted = weighted + rounded(prob) * spread(ref, 2 * HEADS + OWN)
    attended = weighted / total
    for d in range(GROUP):
        pieces_ref[d] = attended


def out_kernel(attended_ref, wout_ref, pieces_ref):
    partial = None
    for j in range(HEADS // 2):
        heads = jnp.concatenate(
            [
                jnp.concatenate(
                    [attended_ref[pl.ds(r * HEADS + 2 * j + k, GROUP, stride=2 * HEADS), :] for r in range(OWN)], axis=0
                )
                for k in range(2)
            ],
            axis=1,
        ).astype(BF16)
        term = jnp.dot(heads, wout_ref[2 * j * DIM : 2 * (j + 1) * DIM, :], preferred_element_type=F32)
        partial = term if partial is None else partial + term
    for d in range(GROUP):
        pieces_ref[d] = partial


def exchange(pieces, axes):
    return lax.all_to_all(pieces, axes, 0, 0, tiled=True)


def per_device(tokens, norm_gain, w_query, w_kv, w_out, key_cache, value_cache, lengths, positions):
    seq_here = key_cache.shape[2]
    width = tokens.shape[1]
    keys, values = key_cache[0], value_cache[0]
    flat = shape(GROUP * PIECE, DIM)
    half = pltpu.VMEM((ROWS, width // 2), F32)
    work = pltpu.VMEM((ROWS // 2, HEADS, 2 * seq_here), F32)
    line = shape(8, DIM)
    pieces, wide, gain, seen, *tables = kernel_call(
        first_kernel,
        [flat, shape(ROWS, width), shape(8, width), shape(ROWS // 2, 2 * seq_here)] + [line] * STEPS,
        *[
            pltpu.with_memory_space_constraint(array, pltpu.HBM)
            for array in (tokens, norm_gain, w_query, w_kv, lengths, positions)
        ],
        scratch=[
            pltpu.VMEM(tokens.shape, BF16),
            pltpu.VMEM(norm_gain.shape, BF16),
            pltpu.VMEM(w_query.shape, BF16),
            pltpu.VMEM(w_kv.shape, BF16),
            pltpu.SMEM(lengths.shape, jnp.int32),
            pltpu.SMEM(positions.shape, jnp.int32),
            half,
            half,
            pltpu.SemaphoreType.DMA((5 + CHUNKS,)),
        ],
        space=pltpu.HBM,
    )
    own, output = [], None
    for step in range(STEPS):
        if step:
            pieces, output = kernel_call(
                next_kernel, [flat, shape(ROWS, width)], sums, wide, gain, w_query, w_kv, after=(other,)
            )
        count = GROUP * GROUP // 2
        block = shape(GROUP // 2, PIECE, DIM)
        if not step:
            parts = exchange(pieces.reshape(GROUP, PIECE, DIM), INNER)
            total = jnp.broadcast_to(jnp.sum(parts, axis=0)[None], (GROUP, PIECE, DIM))
            parts = exchange(total, ("y",))
            other = kernel_call(swap_kernel, shape(2, ROWS // 2, seq_here, DIM), keys, values, after=(parts,))
            parts, other = lax.optimization_barrier((parts, other))
            other = lax.ppermute(other, "core", [(0, 1), (1, 0)])
            outs = [shape(GROUP // 2, 2 * HEADS, DIM), shape(1, PIECE, DIM)]
            pieces, mine = kernel_call(turn_kernel, outs, parts, tables[step])
            queries = exchange(pieces, ("x",))
            pieces = kernel_call(attend_kernel, block, queries, keys, values, other, seen, scratch=[work])
        else:
            parts = exchange(pieces.reshape(GROUP * GROUP, 1, SHARE * DIM), SEQ).reshape(GROUP * PIECE, DIM)
            pieces = kernel_call(turn_shares_kernel, shape(count * SHARE, DIM), parts, tables[step], after=(other,))
            queries = exchange(pieces.reshape(count, 1, SHARE * DIM), ("y", "x")).reshape(count * SHARE, DIM)
            pieces, mine = kernel_call(
                attend_kernel, [block, block], queries, keys, values, other, seen, scratch=[work]
            )
        own.append(mine)
        parts = exchange(pieces, ("x",))
        kept = () if step else (other,)
        pieces = kernel_call(merge_kernel, shape(GROUP * DENSE, DIM), parts, after=kept)
        parts = exchange(pieces.reshape(GROUP, 1, DENSE * DIM), ("y",)).reshape(GROUP * DENSE, DIM)
        pieces = kernel_call(finish_kernel, shape(GROUP, 2 * HEADS, DIM), parts, *own, after=kept)
        attended = exchange(pieces, INNER).reshape(GROUP * 2 * HEADS, DIM)
        sums = exchange(kernel_call(out_kernel, shape(GROUP, ROWS, width), attended, w_out, after=kept), ("heads",))
    return kernel_call(last_kernel, shape(STEPS, ROWS, width), sums, output)


def solution(mesh):
    heads_size, seq_size = mesh.shape["heads"], mesh.shape["seq"]
    devices = mesh.devices.reshape(heads_size, CHIPS_Y, seq_size // CHIPS_Y // 2, 2)
    fine = Mesh(devices, ("heads", "y", "x", "core"))
    in_specs = (
        P(None, SEQ),
        P(SEQ),
        P(SEQ, "heads"),
        P(SEQ, "heads"),
        P("heads", SEQ),
        P("heads", None, SEQ, None),
        P("heads", None, SEQ, None),
        P(),
        P(),
    )
    return jax.shard_map(
        per_device, mesh=fine, in_specs=in_specs, out_specs=P(None, None, SEQ), check_vma=False
    )
```

```python
import functools
import math

import jax
import jax.numpy as jnp
from jax import lax
from jax.experimental import pallas as pl
from jax.experimental.pallas import tpu as pltpu
from jax.sharding import Mesh, PartitionSpec as P

D = 16384
STEPS = 2
EPSILON = 1e-05
ROPE_BASE = 500000.0
FILLER = -3e38
CHIPS_Y = 8
INNER = ("x", "core")
SEQ = ("y", "x", "core")

ROWS = 16
HEADS = 16
DIM = 128
GROUP = 8
OWN = ROWS // GROUP
PIECE = 40
BATCH = 2
CHUNKS = 2
DENSE = 33
CLOSE = 34
SHARE = 5
QUARTER = HEADS // 4
SCALE = 1.0 / math.sqrt(DIM)
F32 = jnp.float32
BF16 = jnp.bfloat16


def kernel_call(body, out_shapes, *args, scratch=(), space=pltpu.VMEM, after=()):
    count = len(args)
    if after:
        inner, args = body, args + tuple(after)

        def body(*refs):
            inner(*refs[:count], *refs[len(args) :])

    single = not isinstance(out_shapes, (list, tuple))
    vmem = pl.BlockSpec(memory_space=pltpu.VMEM)
    return pl.pallas_call(
        body,
        out_shape=out_shapes,
        in_specs=[pl.BlockSpec(memory_space=space)] * len(args),
        out_specs=vmem if single else [vmem] * len(out_shapes),
        scratch_shapes=list(scratch),
        compiler_params=pltpu.CompilerParams(vmem_limit_bytes=16 * 1024 * 1024),
    )(*args)


def shape(*dims):
    return jax.ShapeDtypeStruct(dims, F32)


def core_row(i, core):
    return i // OWN * (2 * OWN) + core * OWN + i % OWN


def project(wide, gain_ref, wq_ref, wkv_ref, pieces_ref, waits=None, shares=False):
    gained = (wide * gain_ref[0:1, :]).astype(BF16)

    def put(head, block):
        for r in range(OWN):
            if not shares:
                start = r * HEADS + head if head < HEADS else 2 * HEADS + (head - HEADS) * OWN + r
            elif head < HEADS:
                start = (r * 4 + head // QUARTER) * GROUP * SHARE + head % QUARTER
            else:
                start = (r * 4 + head - HEADS) * GROUP * SHARE + SHARE - 1
            stride = SHARE if shares else PIECE
            pieces_ref[pl.ds(start, GROUP, stride=stride), :] = block[r * GROUP : (r + 1) * GROUP]

    for j in range(HEADS // 2):
        if waits:
            waits[j]()
        both = jnp.dot(gained, wq_ref[:, 2 * j * DIM : 2 * (j + 1) * DIM], preferred_element_type=F32)
        for k in range(2):
            put(2 * j + k, both[:, k * DIM : (k + 1) * DIM])
    if waits:
        waits[-1]()
    both = jnp.dot(gained, wkv_ref[...], preferred_element_type=F32)
    put(HEADS + 0, both[:, :DIM])
    put(HEADS + 1, both[:, DIM:])
    squares = jnp.broadcast_to(jnp.sum(wide * wide, axis=1, keepdims=True), (ROWS, DIM))
    put(HEADS + 2, squares)
    put(HEADS + 3, jnp.zeros((ROWS, DIM), F32))


def first_kernel(
    tokens_hbm, gain_hbm, wq_hbm, wkv_hbm, lengths_hbm, positions_hbm,
    pieces_ref, wide_ref, gain_ref, seen_ref, *refs,
):
    table_refs, (tokens_ref, gain_in, wq_ref, wkv_ref, lengths_ref, positions_ref, left_ref, right_ref, sems) = (
        refs[:STEPS], refs[STEPS:],
    )
    chunk = wq_ref.shape[1] // CHUNKS
    pairs = [
        (lengths_hbm, lengths_ref),
        (positions_hbm, positions_ref),
        (tokens_hbm, tokens_ref),
        (gain_hbm, gain_in),
        (wkv_hbm, wkv_ref),
    ]
    columns = [pl.ds(c * chunk, chunk) for c in range(CHUNKS)]
    pairs += [(wq_hbm.at[:, c], wq_ref.at[:, c]) for c in columns]
    copies = [pltpu.make_async_copy(a, b, sems.at[i]) for i, (a, b) in enumerate(pairs)]
    for copy in copies[5:] + copies[:5]:
        copy.start()
    inner = lax.axis_index("x") * 2 + lax.axis_index("core")
    core = lax.axis_index("core")
    seq_here = seen_ref.shape[1] // 2
    column = lax.broadcasted_iota(jnp.int32, (1, 2 * seq_here), 1)
    block = lax.axis_index("y") * GROUP + lax.axis_index("x") * 2
    spot = jnp.where(
        column < seq_here, (block + core) * seq_here + column, (block - core) * seq_here + column
    )
    copies[0].wait()
    copies[1].wait()
    for i in range(ROWS // 2):
        seen_ref[i : i + 1, :] = jnp.where(spot < lengths_ref[core_row(i, core)], 1.0, 0.0)
    lane = lax.broadcasted_iota(jnp.int32, (8, DIM), 1)
    line = lax.broadcasted_iota(jnp.int32, (8, DIM), 0)
    index = jnp.where(lane < DIM // 2, lane, lane - DIM // 2).astype(F32)
    freqs = jnp.exp(index * (-2.0 * math.log(ROPE_BASE) / DIM))
    both = (positions_ref[inner * OWN], positions_ref[inner * OWN + 1])
    one = jnp.where(lax.axis_index("y") >= 4, both[1], both[0])
    for step, ref in enumerate(table_refs):
        place = jnp.where(line % 2 == 1, both[1], both[0]) if step == 0 else jnp.broadcast_to(one, line.shape)
        angles = (place + step).astype(F32) * freqs
        sine = jnp.sin(angles)
        cosines = line < OWN if step == 0 else line == 0
        ref[...] = jnp.where(cosines, jnp.cos(angles), jnp.where(lane < DIM // 2, -sine, sine))
    copies[2].wait()
    copies[3].wait()
    width = tokens_ref.shape[1] // 2
    left_ref[...] = tokens_ref[:, :width].astype(F32)
    right_ref[...] = tokens_ref[:, width:].astype(F32)
    wide = jnp.concatenate(
        [
            jnp.concatenate([ref[pl.ds(r, GROUP, stride=OWN), :] for r in range(OWN)], axis=0)
            for ref in (left_ref, right_ref)
        ],
        axis=1,
    )
    wide_ref[...] = wide
    gain_ref[...] = jnp.broadcast_to(gain_in[...].astype(F32).reshape(1, 2 * width), gain_ref.shape)
    waits = [lambda j=j: copies[5 + j * 2 * DIM // chunk].wait() if j * 2 * DIM % chunk == 0 else None for j in range(HEADS // 2)]
    project(wide, gain_ref, wq_ref, wkv_ref, pieces_ref, waits + [copies[4].wait])


def next_kernel(sums_ref, last_ref, gain_ref, wq_ref, wkv_ref, pieces_ref, output_ref):
    output = sums_ref[0]
    for s in range(1, GROUP):
        output = output + sums_ref[s]
    output_ref[...] = output
    wide = (last_ref[...] + output).astype(BF16).astype(F32)
    project(wide, gain_ref, wq_ref, wkv_ref, pieces_ref, shares=True)


def last_kernel(sums_ref, first_ref, result_ref):
    output = sums_ref[0]
    for s in range(1, GROUP):
        output = output + sums_ref[s]
    for step, value in enumerate((first_ref[...], output)):
        for b in range(ROWS):
            at = b % OWN * GROUP + b // OWN
            result_ref[step, b : b + 1, :] = value[at : at + 1, :]


def turn_kernel(parts_ref, table_ref, pieces_ref, own_ref):
    whole = parts_ref[0]
    for s in range(1, GROUP):
        whole = whole + parts_ref[s]
    table = table_ref[...]
    below = whole[2 * HEADS :]
    first = 2 * OWN
    inverse = [lax.rsqrt(below[first + r : first + r + 1] / D + EPSILON) for r in range(OWN)]
    cosine = [table[r : r + 1] for r in range(OWN)]
    sine = [table[OWN + r : OWN + r + 1] for r in range(OWN)]
    blocks = []
    for r in range(OWN):
        scaled = whole[r * HEADS : (r + 1) * HEADS] * inverse[r]
        blocks.append(scaled * cosine[r] + pltpu.roll(scaled, DIM // 2, 1) * sine[r])
    line = lax.broadcasted_iota(jnp.int32, below.shape, 0)
    odd = line % 2 == 1
    scaled = below * jnp.where(odd, inverse[1], inverse[0])
    cosines = jnp.where(line < OWN, jnp.where(odd, cosine[1], cosine[0]), 1.0)
    sines = jnp.where(line < OWN, jnp.where(odd, sine[1], sine[0]), 0.0)
    blocks.append(scaled * cosines + pltpu.roll(scaled, DIM // 2, 1) * sines)
    piece = jnp.concatenate(blocks, axis=0)
    own_ref[0] = piece
    for d in range(pieces_ref.shape[0]):
        pieces_ref[d] = piece[: 2 * HEADS]


def turn_shares_kernel(parts_ref, table_ref, pieces_ref):
    step = GROUP * SHARE
    sums = []
    for t in range(SHARE):
        total = parts_ref[pl.ds(t, GROUP, stride=SHARE), :]
        for k in range(step, parts_ref.shape[0], step):
            total = total + parts_ref[pl.ds(k + t, GROUP, stride=SHARE), :]
        sums.append(jnp.sum(total, axis=0, keepdims=True))
    whole = jnp.concatenate(sums, axis=0)
    turned = whole * table_ref[0:1, :] + pltpu.roll(whole, DIM // 2, 1) * table_ref[1:2, :]
    line = lax.broadcasted_iota(jnp.int32, whole.shape, 0)
    quarter = jnp.broadcast_to(lax.rem(lax.axis_index("y"), 4), whole.shape)
    piece = jnp.where((line < SHARE - 1) | (quarter == 0), turned, whole)
    copies = jnp.concatenate([piece] * GROUP, axis=0)
    for k in range(0, pieces_ref.shape[0], step):
        pieces_ref[k : k + step, :] = copies


def diagonal():
    shape_here = (2 * HEADS, DIM)
    return lax.broadcasted_iota(jnp.int32, shape_here, 0) == lax.broadcasted_iota(jnp.int32, shape_here, 1)


def to_lanes(column):
    return jnp.sum(jnp.where(diagonal(), column, 0.0), axis=0, keepdims=True)


def to_column(line):
    return jnp.sum(jnp.where(diagonal(), line, 0.0), axis=1, keepdims=True)


def joined(top, total):
    lane = lax.broadcasted_iota(jnp.int32, (1, DIM), 1)
    return jnp.where(lane < 2 * HEADS, top, jnp.where(lane < 4 * HEADS, pltpu.roll(total, 2 * HEADS, 1), 0.0))


def swap_kernel(keys_ref, values_ref, other_ref):
    core = lax.axis_index("core")
    for i in range(ROWS // 2):
        b = core_row(i, 1 - core)
        other_ref[0, i] = keys_ref[b].astype(F32)
        other_ref[1, i] = values_ref[b].astype(F32)


def attend_kernel(queries_ref, keys_ref, values_ref, other_ref, seen_ref, pieces_ref, *refs):
    own_ref, work_ref = (None, *refs)[-2:]
    core = lax.axis_index("core")
    seq_here = keys_ref.shape[1]
    halves = (slice(0, seq_here), slice(seq_here, 2 * seq_here))

    def place(i):
        return i // OWN, slice(i % OWN * HEADS, (i % OWN + 1) * HEADS)

    for i in range(ROWS // 2):
        x, heads = place(i)
        if own_ref is None:
            scaled = queries_ref[x, heads, :]
        else:
            starts = [((i % OWN * 4 + quarter) * (GROUP // 2) + x) * SHARE for quarter in range(4)]
            ends = [queries_ref[start + SHARE - 1 : start + SHARE, :] for start in starts]
            inverse = lax.rsqrt(ends[2] / D + EPSILON)
            scaled = jnp.concatenate([queries_ref[start : start + QUARTER, :] for start in starts], axis=0) * inverse
            own_ref[x, heads, :] = scaled
            for k in range(2):
                line = 2 * HEADS + k * OWN + i % OWN
                own_ref[x, line : line + 1, :] = ends[k] * inverse
        queries = scaled.astype(BF16)
        for half, keys in zip(halves, (keys_ref[core_row(i, core)], other_ref[0, i].astype(BF16))):
            work_ref[i, :, half] = lax.dot_general(
                queries, keys, (((1,), (1,)), ((), ())), preferred_element_type=F32
            )
    for c in range(0, ROWS // 2, BATCH):
        scores = work_ref[c : c + BATCH] * SCALE
        seen = jnp.broadcast_to(seen_ref[c : c + BATCH, :][:, None, :], scores.shape) > 0.0
        tops = jnp.max(jnp.where(seen, scores, FILLER), axis=2, keepdims=True)
        probs = jnp.where(seen, jnp.exp(scores - tops), 0.0)
        totals = jnp.sum(probs, axis=2, keepdims=True)
        work_ref[c : c + BATCH] = probs
        for b in range(0, BATCH, OWN):
            top = tops[b : b + OWN].reshape(OWN * HEADS, 1)
            total = totals[b : b + OWN].reshape(OWN * HEADS, 1)
            stats = joined(to_lanes(top), to_lanes(total))
            end = ((c + b) // OWN + 1) * CLOSE
            pieces_ref[end - CLOSE + 2 * HEADS : end, :] = jnp.broadcast_to(stats, (CLOSE - 2 * HEADS, DIM))
    for i in range(ROWS // 2):
        x, heads = place(i)
        own, other = (work_ref[i, :, half].astype(BF16) for half in halves)
        begin = x * CLOSE + heads.start
        pieces_ref[begin : begin + HEADS, :] = jnp.dot(
            own, values_ref[core_row(i, core)], preferred_element_type=F32
        ) + jnp.dot(other, other_ref[1, i].astype(BF16), preferred_element_type=F32)


def merge(weighted, stats):
    top = functools.reduce(jnp.maximum, stats)
    total, whole = None, None
    for part, stat in zip(weighted, stats):
        factor = jnp.exp(stat - top)
        here = factor * pltpu.roll(stat, DIM - 2 * HEADS, 1)
        part = to_column(factor) * part
        total = here if total is None else total + here
        whole = part if whole is None else whole + part
    return top, total, whole


def merge_kernel(parts_ref, pieces_ref):
    top, total, weighted = merge(*zip(*[
        (parts_ref[s : s + 2 * HEADS, :], parts_ref[s + 2 * HEADS : s + 2 * HEADS + 1, :])
        for s in range(0, parts_ref.shape[0], CLOSE)
    ]))
    stats = joined(top, total)
    for d in range(GROUP):
        pieces_ref[d * DENSE : d * DENSE + 2 * HEADS, :] = weighted
        pieces_ref[d * DENSE + 2 * HEADS : (d + 1) * DENSE, :] = stats


def finish_kernel(parts_ref, *refs):
    own_refs, pieces_ref = refs[:-1], refs[-1]
    x = lax.axis_index("x")

    def rounded(value):
        return value.astype(BF16).astype(F32)

    def spread(ref, line):
        return jnp.concatenate(
            [jnp.broadcast_to(rounded(ref[x if ref.shape[0] > 1 else 0, line + r : line + r + 1, :]), (HEADS, DIM)) for r in range(OWN)], axis=0
        )

    top, total, weighted = merge(*zip(*[
        (parts_ref[s * DENSE : s * DENSE + 2 * HEADS, :], parts_ref[s * DENSE + 2 * HEADS : (s + 1) * DENSE, :])
        for s in range(GROUP)
    ]))
    top, total = to_column(top), to_column(total)
    queries = rounded(own_refs[-1][x if own_refs[-1].shape[0] > 1 else 0, : 2 * HEADS, :])
    scores = [jnp.sum(queries * spread(ref, 2 * HEADS), axis=1, keepdims=True) * SCALE for ref in own_refs]
    whole_top = functools.reduce(jnp.maximum, scores, top)
    factor = jnp.exp(top - whole_top)
    total = total * factor
    weighted = weighted * factor
    for score, ref in zip(scores, own_refs):
        prob = jnp.exp(score - whole_top)
        total = total + prob
        weighted = weighted + rounded(prob) * spread(ref, 2 * HEADS + OWN)
    attended = weighted / total
    for d in range(GROUP):
        pieces_ref[d] = attended


def out_kernel(attended_ref, wout_ref, pieces_ref):
    partial = None
    for j in range(HEADS // 2):
        heads = jnp.concatenate(
            [
                jnp.concatenate(
                    [attended_ref[pl.ds(r * HEADS + 2 * j + k, GROUP, stride=2 * HEADS), :] for r in range(OWN)], axis=0
                )
                for k in range(2)
            ],
            axis=1,
        ).astype(BF16)
        term = jnp.dot(heads, wout_ref[2 * j * DIM : 2 * (j + 1) * DIM, :], preferred_element_type=F32)
        partial = term if partial is None else partial + term
    for d in range(GROUP):
        pieces_ref[d] = partial


def exchange(pieces, axes):
    return lax.all_to_all(pieces, axes, 0, 0, tiled=True)


def per_device(tokens, norm_gain, w_query, w_kv, w_out, key_cache, value_cache, lengths, positions):
    seq_here = key_cache.shape[2]
    width = tokens.shape[1]
    keys, values = key_cache[0], value_cache[0]
    flat = shape(GROUP * PIECE, DIM)
    half = pltpu.VMEM((ROWS, width // 2), F32)
    work = pltpu.VMEM((ROWS // 2, HEADS, 2 * seq_here), F32)
    line = shape(8, DIM)
    pieces, wide, gain, seen, *tables = kernel_call(
        first_kernel,
        [flat, shape(ROWS, width), shape(8, width), shape(ROWS // 2, 2 * seq_here)] + [line] * STEPS,
        *[
            pltpu.with_memory_space_constraint(array, pltpu.HBM)
            for array in (tokens, norm_gain, w_query, w_kv, lengths, positions)
        ],
        scratch=[
            pltpu.VMEM(tokens.shape, BF16),
            pltpu.VMEM(norm_gain.shape, BF16),
            pltpu.VMEM(w_query.shape, BF16),
            pltpu.VMEM(w_kv.shape, BF16),
            pltpu.SMEM(lengths.shape, jnp.int32),
            pltpu.SMEM(positions.shape, jnp.int32),
            half,
            half,
            pltpu.SemaphoreType.DMA((5 + CHUNKS,)),
        ],
        space=pltpu.HBM,
    )
    own, output = [], None
    for step in range(STEPS):
        if step:
            pieces, output = kernel_call(
                next_kernel, [flat, shape(ROWS, width)], sums, wide, gain, w_query, w_kv, after=(other,)
            )
        count = GROUP * GROUP // 2
        block = shape(GROUP // 2, PIECE, DIM)
        close = shape(GROUP // 2 * CLOSE, DIM)
        if not step:
            parts = exchange(pieces.reshape(GROUP, PIECE, DIM), INNER)
            total = jnp.broadcast_to(jnp.sum(parts, axis=0)[None], (GROUP, PIECE, DIM))
            parts = exchange(total, ("y",))
            other = kernel_call(swap_kernel, shape(2, ROWS // 2, seq_here, DIM), keys, values, after=(parts,))
            parts, other = lax.optimization_barrier((parts, other))
            other = lax.ppermute(other, "core", [(0, 1), (1, 0)])
            outs = [shape(GROUP // 2, 2 * HEADS, DIM), shape(1, PIECE, DIM)]
            pieces, mine = kernel_call(turn_kernel, outs, parts, tables[step])
            queries = exchange(pieces, ("x",))
            pieces = kernel_call(attend_kernel, close, queries, keys, values, other, seen, scratch=[work])
        else:
            parts = exchange(pieces.reshape(GROUP * GROUP, 1, SHARE * DIM), SEQ).reshape(GROUP * PIECE, DIM)
            pieces = kernel_call(turn_shares_kernel, shape(count * SHARE, DIM), parts, tables[step], after=(other,))
            queries = exchange(pieces.reshape(count, 1, SHARE * DIM), ("y", "x")).reshape(count * SHARE, DIM)
            pieces, mine = kernel_call(
                attend_kernel, [close, block], queries, keys, values, other, seen, scratch=[work]
            )
        own.append(mine)
        parts = exchange(pieces.reshape(GROUP // 2, 1, CLOSE * DIM), ("x",)).reshape(GROUP // 2 * CLOSE, DIM)
        kept = () if step else (other,)
        pieces = kernel_call(merge_kernel, shape(GROUP * DENSE, DIM), parts, after=kept)
        parts = exchange(pieces.reshape(GROUP, 1, DENSE * DIM), ("y",)).reshape(GROUP * DENSE, DIM)
        pieces = kernel_call(finish_kernel, shape(GROUP, 2 * HEADS, DIM), parts, *own, after=kept)
        attended = exchange(pieces, INNER).reshape(GROUP * 2 * HEADS, DIM)
        sums = exchange(kernel_call(out_kernel, shape(GROUP, ROWS, width), attended, w_out, after=kept), ("heads",))
    return kernel_call(last_kernel, shape(STEPS, ROWS, width), sums, output)


def solution(mesh):
    heads_size, seq_size = mesh.shape["heads"], mesh.shape["seq"]
    devices = mesh.devices.reshape(heads_size, CHIPS_Y, seq_size // CHIPS_Y // 2, 2)
    fine = Mesh(devices, ("heads", "y", "x", "core"))
    in_specs = (
        P(None, SEQ),
        P(SEQ),
        P(SEQ, "heads"),
        P(SEQ, "heads"),
        P("heads", SEQ),
        P("heads", None, SEQ, None),
        P("heads", None, SEQ, None),
        P(),
        P(),
    )
    return jax.shard_map(
        per_device, mesh=fine, in_specs=in_specs, out_specs=P(None, None, SEQ), check_vma=False
    )
```
